256 devices in a mesh: species: 128 (over x, z, y), params: 2 (over core).
Axes of the slice: x: 4, y: 4, z: 8, core: 2. Of those that a mesh axis runs over, the one named last changes fastest.
Arguments:
- species_state: float32 [131072], P('species'), may hold values from 0.2 to 2
- sensitivity: float32 [131072, 512], P('species', 'params'), may hold values from -6 to 6
- jacobian_blocks: float32 [1024, 5, 128, 128], P('species'), may hold values from -0.25 to 0.25
- block_columns: int32 [1024, 5], P('species'), may hold values from 0 to 1023, as said below
- block_counts: int32 [1024], P('species'), may hold values from 1 to 5, as said below
- reaction_rows: int32 [131072, 2], P(('species', 'params')), may hold values from 0 to 1023
- stoichiometry: int32 [131072, 2], P(('species', 'params')), may hold values from 1 to 2
- catalyst_device: int32 [131072, 1], P(('species', 'params')), may hold values from 0 to 127; in each aligned block of 512 rows (0 to 511, 512 to 1023, ...) at most 8 rows name the same one
- catalyst_row: int32 [131072], P(('species', 'params')), may hold values from 0 to 1023
- param_index: int32 [131072], P(('species', 'params')), may hold values from 0 to 511
- rate_constant: float32 [131072], P(('species', 'params')), may hold values from 0.05 to 1
Outputs:
- sensitivity_next: float32 [131072, 512], P('species', 'params')
The draws below stay inside these ranges and needn't reach their ends.
Inputs may be any that keep to these rules, and one draw needn't show every extreme that they name: `block_columns`: slot 0 names the block row itself; every other slot names a block within 3 blocks of it. `block_counts`: the leading used slots of each block row. `catalyst_device`: among the 512 reactions of one index pair of species and params, at most 8 name one index of species.
All inputs are finite; a program needn't handle non-finite values.
Results may differ from the reference program's by a relative error of at most 0.0003.
Values sent between devices are 32-bit elements; how exact they have to be, the bound alone decides.
No kernel may reach another device: no remote copies, remote signals or barrier semaphores. Data moves between devices by JAX's collectives and lax.ppermute only.
A program may use at most 64 MiB of HBM per device.

```python
import math
import jax
import jax.numpy as jnp
import numpy as np
from jax import lax

B = 128
P_SIZE = 512
H = 3
NNZ = 5
BLK_DEV = 8
R_DEV = 1024
ROWS_DEV = 1024
NBLK = 1024
NSPEC = 131072
RTOT = 131072
RP = 512
CAP = 8
N_SPECIES = 128


def draw_block_columns(key, part):
    key = jax.random.fold_in(key, 23)
    scores = jax.random.randint(key, (NBLK, 2 * H), 0, 4096) * (2 * H) + jnp.arange(2 * H)[None, :]
    order = jnp.argsort(scores, axis=1)
    candidates = jnp.concatenate([-jnp.arange(1, H + 1), jnp.arange(1, H + 1)])
    offsets = candidates[order[:, :NNZ - 1]]
    block_ids = jnp.arange(NBLK)[:, None]
    forward = block_ids + offsets
    outside = jnp.logical_or(forward < 0, forward >= NBLK)
    columns = jnp.where(outside, block_ids - offsets, forward)
    return jnp.concatenate([block_ids, columns], axis=1).astype(jnp.int32)


def draw_block_counts(key, part):
    key = jax.random.fold_in(key, 11)
    level_key, pick_key, jitter_key = jax.random.split(key, 3)
    groups = NBLK // BLK_DEV
    levels = jax.random.randint(level_key, (groups,), 1, NNZ + 1)
    picked = jax.random.randint(pick_key, (), 0, groups)
    levels = jnp.where(jnp.arange(groups) == picked, NNZ, levels)
    jitter = jax.random.randint(jitter_key, (groups, BLK_DEV), -1, 2)
    counts = jnp.clip(levels[:, None] + jitter, 1, NNZ)
    counts = counts.at[picked, 0].set(NNZ)
    counts = counts.at[(picked + 1) % groups, 0].set(1)
    return counts.reshape(NBLK).astype(jnp.int32)


def set_ends(array, own_key, smallest, largest):
    place = [jax.random.randint(jax.random.fold_in(own_key, axis), (), 0, length) for axis, length in enumerate(array.shape)]
    widest = array.shape.index(max(array.shape))
    next_to = place[:widest] + [(place[widest] + 1) % array.shape[widest]] + place[widest + 1:]
    return array.at[tuple(place)].set(smallest).at[tuple(next_to)].set(largest)


def block_scale(own_key, shape, pieces, least, top_value):
    gain = 1.0
    for axis_at, blocks in pieces:
        heights = jax.random.uniform(jax.random.fold_in(jax.random.fold_in(own_key, 6), axis_at), (blocks,), jnp.float32, least / len(pieces), top_value / len(pieces))
        gain = gain * jnp.repeat(jnp.exp(heights), shape[axis_at] // blocks).reshape((-1,) + (1,) * (len(shape) - 1 - axis_at))
    return gain


def routed_block(rng, own, number, rows, number_of, top, most, slope):
    ranking = jax.random.permutation(rng, number_of)
    packed, common = load_shares(number_of, rows * top, most, slope, True), load_shares(number_of, rows * top, most, slope, False)
    places = jnp.arange(number_of)

    def named(lengths, offset_by):
        used = int((lengths > 0).sum())
        fixed = max(1, used // 4)
        passed = fixed + (places - fixed + offset_by * (used - fixed)) % max(1, number_of - fixed)
        return jnp.zeros((number_of,), jnp.int32).at[ranking[jnp.where(places < fixed, places, passed)]].set(jnp.asarray(lengths, jnp.int32))

    lengths = jnp.where(number % 4 == 0, named(packed, number // 4), named(common, number - number // 4 - 1))
    mixed = jax.random.permutation(jax.random.fold_in(own, 3), number_of)
    source_of, sink = mixed[0:number_of // 2 * 2:2], mixed[1:number_of // 2 * 2:2]
    margin = jnp.minimum(lengths[source_of] - 1, most - lengths[sink]) // 2
    margin = jnp.where((source_of == ranking[0]) | (sink == ranking[0]) | (lengths[sink] == 0), 0, jnp.maximum(margin, 0))
    passed = jax.random.randint(jax.random.fold_in(own, 4), (number_of // 2,), 0, 1 << 20) % (margin + 1)
    lengths = lengths.at[source_of].add(-passed).at[sink].add(passed)
    items = jnp.searchsorted(jnp.cumsum(lengths), jnp.arange(rows * top), side="right").astype(jnp.int32)
    table = items.reshape(top, rows).T
    table = table[jax.random.permutation(jax.random.fold_in(own, 1), rows)]
    offset_by = jax.random.randint(jax.random.fold_in(own, 2), (rows, 1), 0, top)
    return jnp.take_along_axis(table, (jnp.arange(top)[None, :] + offset_by) % top, axis=1)


def load_shares(amount, total, bound, lean, full):
    loads = [(1 << 20) // math.isqrt(rank ** lean) + 1 for rank in range(1, amount + 1)]
    largest = bound if full else min(bound, max(-(-total // amount), total * loads[0] // sum(loads)))
    least = 1 if total - largest >= amount - 1 else 0
    given, surplus = [largest] + [least] * (amount - 1), total - largest - least * (amount - 1)
    while surplus > 0:
        movable = [i for i in range(1, amount) if given[i] < largest] or [i for i in range(1, amount) if given[i] < bound]
        whole, budget = sum([loads[i] for i in movable]), surplus
        for i in movable:
            extra = min(bound - given[i], max(1, budget * loads[i] // whole), surplus)
            given[i] = given[i] + extra
            surplus = surplus - extra
    return np.array(given)


def bell_draw(rng, extent, deviation, most, cuts=(), kind=jnp.bfloat16):
    factor_of = block_scale(rng, extent, cuts, -0.22, 0.18) if cuts else 1.0
    drawn = jax.random.normal(rng, extent, jnp.float32) * deviation * factor_of
    return jnp.minimum(jnp.maximum(drawn, -most), most).astype(kind)


def setup_inputs(seed: int = 0) -> dict:
    streams_of = jax.random.split(jax.random.key(seed), 12)
    species_state = jnp.clip(jnp.exp(math.log(2.0) - 2.3025851 * jax.random.uniform(streams_of[0], (NSPEC,), jnp.float32) ** block_scale(streams_of[0], (NSPEC,), ((0, 128),), -0.2, 0.2)), 0.2, 2.0)
    sensitivity = bell_draw(streams_of[1], (NSPEC, P_SIZE), 1.0, 6.0, ((0, 128), (1, 2)), jnp.float32)
    jacobian_blocks = bell_draw(streams_of[2], (NBLK, NNZ, B, B), (B * NNZ) ** -0.5, 0.25, ((0, 128),), jnp.float32)
    block_columns = draw_block_columns(jax.random.fold_in(streams_of[11], 71), 0)
    block_counts = draw_block_counts(jax.random.fold_in(streams_of[11], 71), 0)
    reaction_rows = set_ends(jax.random.randint(streams_of[5], (RTOT, 2), 0, ROWS_DEV), jax.random.fold_in(streams_of[5], 1), 0, ROWS_DEV - 1).astype(jnp.int32)
    stoichiometry = set_ends(jax.random.randint(streams_of[6], (RTOT, 2), 1, 3), jax.random.fold_in(streams_of[6], 1), 1, 2).astype(jnp.int32)
    catalyst_device_keys = jax.random.split(jax.random.fold_in(streams_of[7], 1), RTOT // RP)
    catalyst_device_turns = jax.random.permutation(jax.random.fold_in(streams_of[7], 3), RTOT // RP)
    catalyst_device = jax.vmap(lambda own, number: routed_block(jax.random.fold_in(streams_of[7], 2), own, number, RP, N_SPECIES, 1, CAP, 1))(catalyst_device_keys, catalyst_device_turns).reshape((RTOT, 1))
    catalyst_row = set_ends(jax.random.randint(streams_of[8], (RTOT,), 0, ROWS_DEV), jax.random.fold_in(streams_of[8], 1), 0, ROWS_DEV - 1).astype(jnp.int32)
    param_index = set_ends(jax.random.randint(streams_of[9], (RTOT,), 0, P_SIZE), jax.random.fold_in(streams_of[9], 1), 0, P_SIZE - 1).astype(jnp.int32)
    rate_constant = jnp.clip(jnp.exp(math.log(1.0) - 2.9957323 * jax.random.uniform(streams_of[10], (RTOT,), jnp.float32) ** block_scale(streams_of[10], (RTOT,), ((0, 256),), -0.2, 0.2)), 0.05, 1.0)
    return {"species_state": species_state, "sensitivity": sensitivity, "jacobian_blocks": jacobian_blocks, "block_columns": block_columns, "block_counts": block_counts, "reaction_rows": reaction_rows, "stoichiometry": stoichiometry, "catalyst_device": catalyst_device, "catalyst_row": catalyst_row, "param_index": param_index, "rate_constant": rate_constant}


step_length = 0.5


def reference(species_state, sensitivity, jacobian_blocks, block_columns, block_counts, reaction_rows, stoichiometry, catalyst_device, catalyst_row, param_index, rate_constant):
    sens_blocks = sensitivity.reshape(NBLK, B, P_SIZE)
    catalyst_global = (catalyst_device[:, 0] * ROWS_DEV + catalyst_row).astype(jnp.int32)
    param_iota = jnp.arange(P_SIZE, dtype=jnp.int32)

    def group_slab(group_index):
        base_block = group_index * BLK_DEV
        rows_here = lax.dynamic_slice_in_dim(jacobian_blocks, base_block, BLK_DEV, 0)
        column_ids = lax.dynamic_slice_in_dim(block_columns, base_block, BLK_DEV, 0)
        counts_here = lax.dynamic_slice_in_dim(block_counts, base_block, BLK_DEV, 0)
        used_slots = (jnp.arange(NNZ, dtype=jnp.int32)[None, :] < counts_here[:, None]).astype(jnp.float32)
        picked = sens_blocks[column_ids]
        band_term = jnp.einsum("rkij,rkjc->ric", rows_here * used_slots[:, :, None, None], picked, precision=lax.Precision.HIGHEST)
        band_term = band_term.reshape(ROWS_DEV, P_SIZE)
        base_row = group_index * ROWS_DEV
        start = group_index * R_DEV
        pair_rows = lax.dynamic_slice_in_dim(reaction_rows, start, R_DEV, 0)
        amounts = lax.dynamic_slice_in_dim(stoichiometry, start, R_DEV, 0).astype(jnp.float32)
        catalyst_here = lax.dynamic_slice_in_dim(catalyst_global, start, R_DEV, 0)
        params_here = lax.dynamic_slice_in_dim(param_index, start, R_DEV, 0)
        constants = lax.dynamic_slice_in_dim(rate_constant, start, R_DEV, 0)
        reactant = pair_rows[:, 0]
        product = pair_rows[:, 1]
        reactant_conc = species_state[base_row + reactant]
        catalyst_conc = species_state[catalyst_here]
        reaction_rate = constants * reactant_conc * catalyst_conc
        chosen = (params_here[:, None] == param_iota[None, :]).astype(jnp.float32)
        growth = (constants * catalyst_conc)[:, None] * sensitivity[base_row + reactant] + (constants * reactant_conc)[:, None] * sensitivity[catalyst_here] + reaction_rate[:, None] * chosen
        reaction_term = jax.ops.segment_sum(amounts[:, 1:2] * growth, product, num_segments=ROWS_DEV) - jax.ops.segment_sum(amounts[:, 0:1] * growth, reactant, num_segments=ROWS_DEV)
        own_rows = lax.dynamic_slice_in_dim(sensitivity, base_row, ROWS_DEV, 0)
        return own_rows + step_length * (band_term + reaction_term)

    slabs = lax.map(group_slab, jnp.arange(N_SPECIES, dtype=jnp.int32))
    return slabs.reshape(NSPEC, P_SIZE)
```

```python
import functools

import jax
import jax.numpy as jnp
from jax import lax
from jax.experimental import pallas as pl
from jax.experimental.pallas import tpu as pltpu
from jax.sharding import PartitionSpec as P

H = 3
CHAIN = 8
STRIDE = 4
SLOTS = 12
FIRST = 8
REST = SLOTS - FIRST
LINES = 2 * SLOTS + 1
SPAN = 1028
RANKS = 16
DIRECT = 16
FLAG = 32
NONE = 127
VMEM_LIMIT = 24 * 1024 * 1024

step_length = 0.5
f32 = jnp.float32
bf16 = jnp.bfloat16
i32 = jnp.int32


def nt(a, b):
    return lax.dot_general(a, b, (((1,), (1,)), ((), ())), preferred_element_type=f32)


def nn(a, b, precision=None):
    return jnp.dot(a, b, preferred_element_type=f32, precision=precision)


def iota(shape, dim):
    return lax.broadcasted_iota(i32, shape, dim)


def halves(x):
    high = x.astype(bf16)
    return high, (x - high.astype(f32)).astype(bf16)


def split_int(x, base):
    high = jnp.floor(x * (1.0 / base))
    return high, x - base * high


def pack_kernel(rows_ref, amounts_ref, owner_ref, row_ref, param_ref, constant_ref, out_ref):
    out_ref[0:2, :] = rows_ref[...].astype(f32)
    out_ref[2:4, :] = amounts_ref[...].astype(f32)
    out_ref[4:5, :] = owner_ref[...].astype(f32)
    out_ref[5:6, :] = row_ref[...].astype(f32)
    out_ref[6:7, :] = param_ref[...].astype(f32)
    out_ref[7:8, :] = constant_ref[...]


def pack(rows_pair, stoichiometry, owner, row, param, constant):
    count = constant.shape[0]
    return pl.pallas_call(
        pack_kernel,
        out_shape=jax.ShapeDtypeStruct((8, count), f32),
        name="pack",
    )(
        rows_pair.T,
        stoichiometry.T,
        owner.T,
        row.reshape(1, count),
        param.reshape(1, count),
        constant.reshape(1, count),
    )


def table_kernel(own_ref, state_ref, out_ref):
    rows, width = own_ref.shape
    for half in range(2):
        out_ref[pl.ds(half, rows, stride=2), :] = own_ref[:, half * 128 : half * 128 + 128]
    out_ref[2 * rows :, :] = state_ref[...]


def make_table(own, state):
    rows = own.shape[0]
    return pl.pallas_call(
        table_kernel,
        out_shape=jax.ShapeDtypeStruct((2 * rows + state.shape[0], 128), f32),
        compiler_params=pltpu.CompilerParams(vmem_limit_bytes=VMEM_LIMIT),
        name="table",
    )(own, state)


def plan_kernel(meta_ref, request_ref, plan_ref):
    count = meta_ref.shape[1]
    devices = request_ref.shape[0]
    owner = meta_ref[4:5, :]
    row = meta_ref[5:6, :]
    owner_hot = (iota((devices, count), 0) == owner.astype(i32)).astype(bf16)
    before = (iota((count, count), 0) < iota((count, count), 1)).astype(bf16)
    earlier = nn(owner_hot, before)
    rank = jnp.sum(earlier * owner_hot.astype(f32), axis=0, keepdims=True)
    load = nt(jnp.ones((8, count), bf16), owner_hot)

    lane = iota((8, devices), 1)
    place = (lane // STRIDE) % CHAIN
    zero = jnp.zeros((8, devices), f32)
    room = f32(SLOTS)
    late, own, ahead, left = zero, zero, zero, zero
    for z in range(CHAIN):
        here = place == z
        late = jnp.where(here, jnp.minimum(pltpu.roll(left, STRIDE, 1), room), late)
        mine = load - ahead
        own = jnp.where(here, jnp.minimum(mine, room - late), own)
        left = jnp.where(here, mine - own, left)
        spare = pltpu.roll(room - late - own, STRIDE, 1)
        ahead = jnp.where(place == z + 1, jnp.minimum(load, spare), ahead)
    late_next = jnp.where(place < CHAIN - 1, pltpu.roll(late, devices - STRIDE, 1), 0.0)
    start_ahead = pltpu.roll(late + own, STRIDE, 1)
    end_own = ahead + own
    end_late = end_own + late_next
    overflow = jnp.sum(load - end_late, axis=1, keepdims=True)

    line = iota((8, devices), 0)
    table = zero
    for k, values in enumerate((ahead, end_own, end_late, start_ahead, late)):
        table = jnp.where(line == k, values, table)
    looked = nn(table.astype(bf16), owner_hot)
    ahead_q, end_own_q, end_late_q = looked[0:1], looked[1:2], looked[2:3]
    start_ahead_q, late_q = looked[3:4], looked[4:5]
    is_ahead = rank < ahead_q
    is_own = rank < end_own_q
    is_late = rank < end_late_q
    slot = jnp.where(
        is_ahead,
        start_ahead_q + rank,
        jnp.where(
            is_own,
            late_q + rank - ahead_q,
            jnp.where(is_late, rank - end_own_q, f32(NONE)),
        ),
    )
    shift = jnp.where(
        is_ahead, f32(-STRIDE), jnp.where(is_own, 0.0, jnp.where(is_late, f32(STRIDE), 0.0))
    )
    part = jnp.where(is_ahead, 2.0, jnp.where(is_own, 0.0, jnp.where(is_late, 1.0, 0.0)))
    carrier = owner + shift
    entry = part * f32(SPAN) + row
    carrier_hot = (iota((devices, count), 0) == carrier.astype(i32)).astype(bf16)
    slot_line = iota((128, count), 0)
    slot_hot = jnp.logical_and(slot_line == slot.astype(i32), slot_line < SLOTS)
    rank_hot = slot_line == rank.astype(i32) + DIRECT
    entry_high, entry_low = split_int(entry, 64.0)
    row_high, row_low = split_int(row, 64.0)

    def listed(hot, places, values):
        return nt(hot, jnp.where(places, values, 0.0).astype(bf16))

    request = 64.0 * (
        listed(carrier_hot, slot_hot, entry_high) + listed(owner_hot, rank_hot, row_high)
    )
    request = request + (
        listed(carrier_hot, slot_hot, entry_low) + listed(owner_hot, rank_hot, row_low)
    )
    lane_out = iota((devices, 128), 1)
    request_ref[...] = jnp.where(lane_out == FLAG, overflow[0:1, 0:1], request)
    line_out = iota((8, count), 0)
    plan = jnp.zeros((8, count), f32)
    for k, values in enumerate((carrier, slot, rank)):
        plan = jnp.where(line_out == k, values, plan)
    plan_ref[...] = plan


def make_plan(meta, devices):
    count = meta.shape[1]
    return pl.pallas_call(
        plan_kernel,
        out_shape=(
            jax.ShapeDtypeStruct((devices, 128), f32),
            jax.ShapeDtypeStruct((8, count), f32),
        ),
        compiler_params=pltpu.CompilerParams(vmem_limit_bytes=VMEM_LIMIT),
        cost_estimate=pl.CostEstimate(flops=10**9, bytes_accessed=200000, transcendentals=0),
        name="plan",
    )(meta)


def gather_kernel(list_ref, state_ref, own_ref, minus_ref, plus_ref, out_ref, table, sems):
    step = pl.program_id(0)
    lines = own_ref.shape[0]
    groups = out_ref.shape[0] // (8 * LINES)

    @pl.when(step == 0)
    def _():
        copies = [
            pltpu.make_async_copy(part, table.at[pl.ds(k * lines, lines)], sems.at[k])
            for k, part in enumerate((own_ref, minus_ref, plus_ref))
        ]
        for copy in copies:
            copy.start()
        for copy in copies:
            copy.wait()

    lane = iota((1, 128), 1)

    def eight(group, carry):
        start = pl.multiple_of(group * (8 * LINES), 8)
        for k in range(8):
            asker = (step * groups + group) * 8 + k
            states = jnp.zeros((1, 128), f32)
            for s in range(SLOTS):
                entry = list_ref[asker, s]
                out_ref[pl.ds(start + k * LINES + 2 * s, 2), :] = table[
                    pl.ds(pl.multiple_of(2 * entry, 2), 2), :
                ]
                states = jnp.where(lane == s, state_ref[entry], states)
            out_ref[pl.ds(start + k * LINES + 2 * SLOTS, 1), :] = states
        return carry

    lax.fori_loop(0, groups, eight, 0)


def gather_rows(lists, states, own, minus, plus):
    devices = lists.shape[0]
    chunk = 32
    smem = pl.BlockSpec(memory_space=pltpu.SMEM)
    return pl.pallas_call(
        gather_kernel,
        grid=(devices // chunk,),
        in_specs=[smem, smem] + [pl.BlockSpec(memory_space=pl.ANY)] * 3,
        out_specs=pl.BlockSpec((chunk * LINES, 128), lambda i: (i, 0)),
        out_shape=jax.ShapeDtypeStruct((devices * LINES, 128), f32),
        scratch_shapes=[pltpu.VMEM((3 * own.shape[0], 128), f32), pltpu.SemaphoreType.DMA((3,))],
        compiler_params=pltpu.CompilerParams(vmem_limit_bytes=VMEM_LIMIT),
        cost_estimate=pl.CostEstimate(flops=0, bytes_accessed=8 * 10**6, transcendentals=0),
        name="gather_rows",
    )(lists, states, own, minus, plus)


def slots_kernel(
    start_ref, meta_ref, plan_ref, near_ref, own_ref, weight_ref, scale_ref, local_ref, high, low
):
    count = meta_ref.shape[1]
    rows, total = weight_ref.shape
    width = own_ref.shape[1]
    carrier = plan_ref[0:1, :]
    slot = plan_ref[1:2, :]
    pair = jnp.floor(carrier * 0.5)
    odd = carrier - 2.0 * pair
    key = pair * (2 * SLOTS) + jnp.where(
        slot < FIRST, odd * FIRST + slot, odd * REST + slot + (2 * FIRST - FIRST)
    )
    key = jnp.where(slot < SLOTS, key, -1.0).astype(i32)
    reactant, product = meta_ref[0:1, :], meta_ref[1:2, :]
    param, constant = meta_ref[6:7, :], meta_ref[7:8, :]
    near = near_ref[8:9, :]
    scaled = constant * near
    a_high, a_low = split_int(reactant, 32.0)
    c_high, c_low = split_int(product, 32.0)
    line = iota((8, count), 0)
    packed = jnp.zeros((8, count), f32)
    for k, values in enumerate(
        (a_high, a_low, c_high, c_low, meta_ref[2:3, :], meta_ref[3:4, :])
    ):
        packed = jnp.where(line == k, values, packed)
    packed = packed.astype(bf16)
    high_part, low_part = halves(own_ref[...])
    high[...] = high_part
    low[...] = low_part
    block = 256
    for start in range(0, total, block):
        hot = iota((block, count), 0) + start == key
        found = nt(packed, jnp.where(hot, 1.0, 0.0).astype(bf16))
        a = (32.0 * found[0:1] + found[1:2]).astype(i32)
        c = (32.0 * found[2:3] + found[3:4]).astype(i32)
        species = iota((rows, block), 0)
        weight = jnp.where(species == c, found[5:6], 0.0) - jnp.where(
            species == a, found[4:5], 0.0
        )
        weight_ref[:, start : start + block] = weight.astype(bf16)

        def column(values):
            return jnp.sum(jnp.where(hot, values, 0.0), axis=1, keepdims=True)

        scale = column(scaled)
        scale_ref[start : start + block, :] = jnp.broadcast_to(scale, (block, 128))
        from_row = (iota((block, rows), 1) == column(reactant).astype(i32)).astype(bf16)
        chosen = iota((block, width), 1) + start_ref[0] == column(param).astype(i32)
        local_ref[start : start + block, :] = column(constant) * (
            nn(from_row, high[...]) + nn(from_row, low[...])
        ) + jnp.where(chosen, scale, 0.0)


def make_slots(start, meta, plan, near, own, devices):
    total = devices * SLOTS
    rows, width = own.shape
    vmem = pl.BlockSpec(memory_space=pltpu.VMEM)
    return pl.pallas_call(
        slots_kernel,
        in_specs=[pl.BlockSpec(memory_space=pltpu.SMEM)] + [vmem] * 4,
        out_shape=(
            jax.ShapeDtypeStruct((rows, total), bf16),
            jax.ShapeDtypeStruct((total, 128), f32),
            jax.ShapeDtypeStruct((total, width), f32),
        ),
        scratch_shapes=[pltpu.VMEM((rows, width), bf16)] * 2,
        compiler_params=pltpu.CompilerParams(vmem_limit_bytes=VMEM_LIMIT),
        cost_estimate=pl.CostEstimate(flops=4 * 10**9, bytes_accessed=5 * 10**6, transcendentals=0),
        name="slots",
    )(start, meta, plan, near, own)


def near_kernel(meta_ref, state_ref, out_ref):
    count = meta_ref.shape[1]
    high, low = split_int(meta_ref[0:1, :], 128.0)
    low_hot = (iota((128, count), 0) == low.astype(i32)).astype(f32)
    columns = nn(state_ref[...], low_hot, lax.Precision.HIGHEST)
    picked = jnp.where(iota((8, count), 0) == high.astype(i32), columns, 0.0)
    out_ref[0:8, :] = picked
    out_ref[8:16, :] = jnp.broadcast_to(jnp.sum(picked, axis=0, keepdims=True), (8, count))


def near_state(meta, state):
    return pl.pallas_call(
        near_kernel,
        out_shape=jax.ShapeDtypeStruct((16, meta.shape[1]), f32),
        compiler_params=pltpu.CompilerParams(vmem_limit_bytes=VMEM_LIMIT),
        name="near_state",
    )(meta, state)


def band_kernel(
    columns_ref, counts_ref, own_ref, before_ref, after_ref, blocks_ref, out_ref, high, low
):
    step = pl.program_id(0)
    rows, width = own_ref.shape
    per_step, _, size, _ = blocks_ref.shape
    edge = before_ref.shape[0]

    @pl.when(step == 0)
    def _():
        for ref, at in ((before_ref, 0), (own_ref, edge), (after_ref, edge + rows)):
            high_part, low_part = halves(ref[...])
            high[at : at + ref.shape[0], :] = high_part
            low[at : at + ref.shape[0], :] = low_part

    for r in range(per_step):
        place = step * per_step + r

        def add_slot(k, sum_so_far):
            at = pl.multiple_of(columns_ref[place, k] * size, size)
            block_high, block_low = halves(blocks_ref[r, k])
            rows_high = high[pl.ds(at, size), :]
            rows_low = low[pl.ds(at, size), :]
            return sum_so_far + (
                nn(block_high, rows_high) + (nn(block_low, rows_high) + nn(block_high, rows_low))
            )

        band = lax.fori_loop(0, counts_ref[place], add_slot, jnp.zeros((size, width), f32))
        at = pl.multiple_of(place * size, size)
        out_ref[r * size : (r + 1) * size, :] = own_ref[pl.ds(at, size), :] + step_length * band


def band_terms(columns, counts, own, before, after, blocks):
    rows, width = own.shape
    block_rows, slots, size, _ = blocks.shape
    per_step = 2
    edge = before.shape[0]

    def whole(x):
        return pl.BlockSpec(x.shape, lambda i: (0,) * x.ndim)

    smem = pl.BlockSpec(memory_space=pltpu.SMEM)
    return pl.pallas_call(
        band_kernel,
        grid=(block_rows // per_step,),
        in_specs=[smem, smem]
        + [whole(x) for x in (own, before, after)]
        + [pl.BlockSpec((per_step, slots, size, size), lambda i: (i, 0, 0, 0))],
        out_specs=pl.BlockSpec((per_step * size, width), lambda i: (i, 0)),
        out_shape=jax.ShapeDtypeStruct((rows, width), f32),
        scratch_shapes=[pltpu.VMEM((rows + 2 * edge, width), bf16)] * 2,
        compiler_params=pltpu.CompilerParams(vmem_limit_bytes=VMEM_LIMIT),
        cost_estimate=pl.CostEstimate(
            flops=3 * 10**9, bytes_accessed=7 * 10**6, transcendentals=0
        ),
        name="band_terms",
    )(columns, counts, own, before, after, blocks)


def tail_kernel(far_ref, scale_ref, local_ref, weight_ref, base_ref, out_ref, mixed, high, low):
    lanes = far_ref.shape[1]
    pairs = far_ref.shape[0] // (2 * LINES)

    @pl.when(pl.program_id(0) == 0)
    def _():
        lane, line = iota((8, lanes), 1), iota((8, lanes), 0)
        upper = line < REST

        def four(group, carry):
            for k in range(4):
                at = pl.multiple_of(group * (8 * LINES), 8) + k * 2 * LINES
                to = pl.multiple_of(group * (8 * SLOTS), 8) + k * 2 * SLOTS
                following = at + LINES
                even_states = jnp.broadcast_to(far_ref[pl.ds(at + 2 * SLOTS, 1), :], (8, lanes))
                odd_states = jnp.broadcast_to(
                    far_ref[pl.ds(following + 2 * SLOTS, 1), :], (8, lanes)
                )
                states = (
                    jnp.where(lane == line, even_states, 0.0),
                    jnp.where(lane == line, odd_states, 0.0),
                    jnp.where(
                        upper,
                        jnp.where(lane == line + FIRST, even_states, 0.0),
                        jnp.where(lane == line + FIRST - REST, odd_states, 0.0),
                    ),
                )
                for half in range(2):
                    values = (
                        far_ref[pl.ds(at + half, 8, stride=2), :],
                        far_ref[pl.ds(following + half, 8, stride=2), :],
                        jnp.where(
                            upper,
                            far_ref[pl.ds(at + 2 * FIRST + half, 8, stride=2), :],
                            far_ref[pl.ds(following + 2 * (FIRST - REST) + half, 8, stride=2), :],
                        ),
                    )
                    columns = slice(half * lanes, (half + 1) * lanes)
                    for j in range(3):
                        state = jnp.sum(states[j], axis=1, keepdims=True)
                        place = pl.ds(to + 8 * j, 8)
                        mixed[place, columns] = (
                            values[j] * scale_ref[place, :] + state * local_ref[place, columns]
                        )
            return carry

        lax.fori_loop(0, pairs // 4, four, 0)
        high_part, low_part = halves(mixed[...])
        high[...] = high_part
        low[...] = low_part

    total = nn(weight_ref[...], high[...]) + nn(weight_ref[...], low[...])
    out_ref[...] = base_ref[...] + step_length * total


def add_far(far, scale, local, weight, base):
    rows, total = weight.shape
    width = base.shape[1]
    block = 256

    def whole(x):
        return pl.BlockSpec(x.shape, lambda i: (0,) * x.ndim)

    return pl.pallas_call(
        tail_kernel,
        grid=(rows // block,),
        in_specs=[
            whole(far),
            whole(scale),
            whole(local),
            pl.BlockSpec((block, total), lambda i: (i, 0)),
            pl.BlockSpec((block, width), lambda i: (i, 0)),
        ],
        out_specs=pl.BlockSpec((block, width), lambda i: (i, 0)),
        out_shape=jax.ShapeDtypeStruct((rows, width), f32),
        scratch_shapes=[pltpu.VMEM((total, width), f32)]
        + [pltpu.VMEM((total, width), bf16)] * 2,
        compiler_params=pltpu.CompilerParams(vmem_limit_bytes=VMEM_LIMIT),
        cost_estimate=pl.CostEstimate(
            flops=2 * 10**9, bytes_accessed=8 * 10**6, transcendentals=0
        ),
        name="add_far",
    )(far, scale, local, weight, base)


def exchange(x):
    return lax.all_to_all(x, "species", split_axis=0, concat_axis=0, tiled=True)


def add_overflow(result, start, meta, plan, near, direct, own, state):
    rows = exchange(own[direct])
    states = exchange(state[direct])
    owner = meta[4].astype(i32)
    rank = plan[2].astype(i32)
    reactant = meta[0].astype(i32)
    product = meta[1].astype(i32)
    constant = jnp.where(plan[1] == NONE, meta[7], 0.0)
    chosen = meta[6].astype(i32)[:, None] - start == iota((1, own.shape[1]), 1)
    growth = (constant * states[owner, rank])[:, None] * (
        own[reactant] + jnp.where(chosen, near[8][:, None], 0.0)
    ) + (constant * near[8])[:, None] * rows[owner, rank]
    result = result.at[product].add(step_length * meta[3][:, None] * growth)
    return result.at[reactant].add(-step_length * meta[2][:, None] * growth)


def along_z(devices, step):
    moved = []
    for i in range(devices):
        z = i // STRIDE % CHAIN
        moved.append((i, i + ((z + step) % CHAIN - z) * STRIDE))
    return moved


def body(
    species_state,
    sensitivity,
    jacobian_blocks,
    block_columns,
    block_counts,
    reaction_rows,
    stoichiometry,
    catalyst_device,
    catalyst_row,
    param_index,
    rate_constant,
):
    devices = lax.axis_size("species")
    rows, width = sensitivity.shape
    block_rows, _, size, _ = jacobian_blocks.shape
    edge = H * size
    ends = devices - 1

    local_meta = pack(
        reaction_rows, stoichiometry, catalyst_device, catalyst_row, param_index, rate_constant
    )
    other_meta = lax.ppermute(local_meta, "params", [(0, 1), (1, 0)])
    meta = jnp.concatenate([local_meta, other_meta], axis=1)
    state_table = species_state.reshape(-1, 128)
    table = make_table(sensitivity, state_table)
    minus = lax.ppermute(table, "species", along_z(devices, 1))
    plus = lax.ppermute(table, "species", along_z(devices, -1))

    request, plan = make_plan(meta, devices)
    asked = exchange(request)
    lists = asked[:, :SLOTS].astype(i32)
    padding = jnp.zeros((SPAN - rows,), f32)
    states = jnp.concatenate(
        [
            piece
            for lines in (state_table, minus[2 * rows :], plus[2 * rows :])
            for piece in (lines.reshape(-1), padding)
        ]
    )
    message = gather_rows(lists, states, table, minus, plus)
    far = exchange(message.reshape(devices, 1, LINES * 128)).reshape(-1, 128)

    own, _ = lax.optimization_barrier((sensitivity, message))
    before = lax.ppermute(own[rows - edge :], "species", [(i, i + 1) for i in range(ends)])
    after = lax.ppermute(own[:edge], "species", [(i + 1, i) for i in range(ends)])
    columns = block_columns - lax.axis_index("species") * block_rows + H
    near = near_state(meta, state_table)
    start = (lax.axis_index("params") * width).astype(i32).reshape(1)
    weight, scale, local = make_slots(start, meta, plan, near, own, devices)
    base = band_terms(columns, block_counts, own, before, after, jacobian_blocks)
    result = add_far(far, scale, local, weight, base)
    direct = asked[:, DIRECT : DIRECT + RANKS].astype(i32)
    return lax.cond(
        jnp.any(asked[:, FLAG] > 0),
        lambda x: add_overflow(
            x, start, meta, plan, near, direct, sensitivity, species_state
        ),
        lambda x: x,
        result,
    )


def solution(mesh):
    placed = (
        P("species"),
        P("species", "params"),
        P("species", None, None, None),
        P("species", None),
        P("species"),
        P(("species", "params"), None),
        P(("species", "params"), None),
        P(("species", "params"), None),
        P(("species", "params")),
        P(("species", "params")),
        P(("species", "params")),
    )
    return jax.shard_map(
        body, mesh=mesh, in_specs=placed, out_specs=P("species", "params"), check_vma=False
    )
```

```python
import functools

import jax
import jax.numpy as jnp
from jax import lax
from jax.experimental import pallas as pl
from jax.experimental.pallas import tpu as pltpu
from jax.sharding import PartitionSpec as P

H = 3
CHAIN = 32
STRIDE = 4
SLOTS = 11
FIRST = 8
REST = SLOTS - FIRST
PAIR = 24
LINES = 2 * SLOTS + 1
SPAN = 1028
RANKS = 16
DIRECT = 16
FLAG = 32
NONE = 127
VMEM_LIMIT = 24 * 1024 * 1024
VMEM_WHOLE = 60 * 1024 * 1024

step_length = 0.5
f32 = jnp.float32
bf16 = jnp.bfloat16
i32 = jnp.int32


def nt(a, b):
    return lax.dot_general(a, b, (((1,), (1,)), ((), ())), preferred_element_type=f32)


def nn(a, b, precision=None):
    return jnp.dot(a, b, preferred_element_type=f32, precision=precision)


def iota(shape, dim):
    return lax.broadcasted_iota(i32, shape, dim)


def halves(x):
    high = x.astype(bf16)
    return high, (x - high.astype(f32)).astype(bf16)


def split_int(x, base):
    high = jnp.floor(x * (1.0 / base))
    return high, x - base * high


def placed(device):
    return (device % STRIDE) * CHAIN + device // STRIDE


def pack_kernel(rows_ref, amounts_ref, owner_ref, row_ref, param_ref, constant_ref, out_ref):
    out_ref[0:2, :] = rows_ref[...].astype(f32)
    out_ref[2:4, :] = amounts_ref[...].astype(f32)
    out_ref[4:5, :] = owner_ref[...].astype(f32)
    out_ref[5:6, :] = row_ref[...].astype(f32)
    out_ref[6:7, :] = param_ref[...].astype(f32)
    out_ref[7:8, :] = constant_ref[...]


def pack(rows_pair, stoichiometry, owner, row, param, constant):
    count = constant.shape[0]
    return pl.pallas_call(
        pack_kernel,
        out_shape=jax.ShapeDtypeStruct((8, count), f32),
        name="pack",
    )(
        rows_pair.T,
        stoichiometry.T,
        owner.T,
        row.reshape(1, count),
        param.reshape(1, count),
        constant.reshape(1, count),
    )


def table_kernel(own_ref, state_ref, out_ref):
    rows, width = own_ref.shape
    for half in range(2):
        out_ref[pl.ds(half, rows, stride=2), :] = own_ref[:, half * 128 : half * 128 + 128]
    out_ref[2 * rows :, :] = state_ref[...]


def make_table(own, state):
    rows = own.shape[0]
    return pl.pallas_call(
        table_kernel,
        out_shape=jax.ShapeDtypeStruct((2 * rows + state.shape[0], 128), f32),
        compiler_params=pltpu.CompilerParams(vmem_limit_bytes=VMEM_LIMIT),
        name="table",
    )(own, state)


def plan_kernel(local_ref, other_ref, request_ref, plan_ref, meta_ref):
    count = meta_ref.shape[1]
    devices = request_ref.shape[0]
    meta_ref[:, : count // 2] = local_ref[...]
    meta_ref[:, count // 2 :] = other_ref[...]
    owner = meta_ref[4:5, :]
    row = meta_ref[5:6, :]
    owner_hot = (iota((devices, count), 0) == owner.astype(i32)).astype(bf16)
    before = (iota((count, count), 0) < iota((count, count), 1)).astype(bf16)
    earlier = nn(owner_hot, before)
    rank = jnp.sum(earlier * owner_hot.astype(f32), axis=0, keepdims=True)
    load = nt(jnp.ones((8, count), bf16), owner_hot)

    spread = (CHAIN * 8, devices)
    held = jnp.where(
        iota(spread, 1) // STRIDE == iota(spread, 0) // 8, load[0:1, :], 0.0
    )
    square = (devices, 128)
    loads = nn(
        held.astype(bf16), (iota(square, 0) % STRIDE == iota(square, 1)).astype(bf16)
    )
    zero = jnp.zeros((8, 128), f32)
    room = f32(SLOTS)
    late, own, ahead = [], [], [zero]
    left = zero
    for z in range(CHAIN):
        here = loads[8 * z : 8 * z + 8]
        late.append(jnp.minimum(left, room))
        mine = here - ahead[z]
        own.append(jnp.minimum(mine, room - late[z]))
        left = mine - own[z]
        if z + 1 < CHAIN:
            ahead.append(
                jnp.minimum(loads[8 * z + 8 : 8 * z + 16], room - late[z] - own[z])
            )
    late.append(zero)
    end_own = [ahead[z] + own[z] for z in range(CHAIN)]
    end_late = [end_own[z] + late[z + 1] for z in range(CHAIN)]
    start_ahead = [zero] + [late[z] + own[z] for z in range(CHAIN - 1)]
    missed = zero
    for z in range(CHAIN):
        missed = missed + (loads[8 * z : 8 * z + 8] - end_late[z])
    overflow = jnp.sum(missed, axis=1, keepdims=True)

    line = iota((8, 128), 0)
    tiles = []
    for values in (ahead, end_own, end_late, start_ahead, late):
        for start in range(0, CHAIN, 8):
            tile = values[start]
            for k in range(1, 8):
                tile = jnp.where(line == k, values[start + k], tile)
            tiles.append(tile)
    place = placed(owner.astype(i32))
    chain_hot = (iota((128, count), 0) == place // CHAIN).astype(bf16)
    looked = nn(jnp.concatenate(tiles, axis=0).astype(bf16), chain_hot)
    at_place = iota((CHAIN, count), 0) == place % CHAIN
    ahead_q, end_own_q, end_late_q, start_ahead_q, late_q = [
        jnp.sum(
            jnp.where(at_place, looked[k * CHAIN : (k + 1) * CHAIN], 0.0), axis=0, keepdims=True
        )
        for k in range(5)
    ]
    is_ahead = rank < ahead_q
    is_own = rank < end_own_q
    is_late = rank < end_late_q
    slot = jnp.where(
        is_ahead,
        start_ahead_q + rank,
        jnp.where(
            is_own,
            late_q + rank - ahead_q,
            jnp.where(is_late, rank - end_own_q, f32(NONE)),
        ),
    )
    shift = jnp.where(is_ahead, -1.0, jnp.where(is_own, 0.0, jnp.where(is_late, 1.0, 0.0)))
    part = jnp.where(is_ahead, 2.0, jnp.where(is_own, 0.0, jnp.where(is_late, 1.0, 0.0)))
    carrier = owner + STRIDE * shift
    entry = part * f32(SPAN) + row
    carrier_hot = (iota((devices, count), 0) == carrier.astype(i32)).astype(bf16)
    slot_line = iota((128, count), 0)
    slot_hot = jnp.logical_and(slot_line == slot.astype(i32), slot_line < SLOTS)
    rank_hot = slot_line == rank.astype(i32) + DIRECT
    entry_high, entry_low = split_int(entry, 64.0)
    row_high, row_low = split_int(row, 64.0)

    def listed(hot, places, values):
        return nt(hot, jnp.where(places, values, 0.0).astype(bf16))

    request = 64.0 * (
        listed(carrier_hot, slot_hot, entry_high) + listed(owner_hot, rank_hot, row_high)
    )
    request = request + (
        listed(carrier_hot, slot_hot, entry_low) + listed(owner_hot, rank_hot, row_low)
    )
    lane_out = iota((devices, 128), 1)
    request_ref[...] = jnp.where(lane_out == FLAG, overflow[0:1, 0:1], request)
    line_out = iota((8, count), 0)
    plan = jnp.zeros((8, count), f32)
    for k, values in enumerate((carrier, slot, rank)):
        plan = jnp.where(line_out == k, values, plan)
    plan_ref[...] = plan


def make_plan(local, other, devices):
    count = 2 * local.shape[1]
    return pl.pallas_call(
        plan_kernel,
        out_shape=(
            jax.ShapeDtypeStruct((devices, 128), f32),
            jax.ShapeDtypeStruct((8, count), f32),
            jax.ShapeDtypeStruct((8, count), f32),
        ),
        compiler_params=pltpu.CompilerParams(vmem_limit_bytes=VMEM_LIMIT),
        cost_estimate=pl.CostEstimate(flops=10**9, bytes_accessed=200000, transcendentals=0),
        name="plan",
    )(local, other)


def gather_kernel(list_ref, state_ref, own_ref, minus_ref, plus_ref, out_ref, table, sems):
    step = pl.program_id(0)
    lines = own_ref.shape[0]
    groups = out_ref.shape[0] // (8 * LINES)

    @pl.when(step == 0)
    def _():
        copies = [
            pltpu.make_async_copy(part, table.at[pl.ds(k * lines, lines)], sems.at[k])
            for k, part in enumerate((own_ref, minus_ref, plus_ref))
        ]
        for copy in copies:
            copy.start()
        for copy in copies:
            copy.wait()

    lane = iota((1, 128), 1)

    def eight(group, carry):
        start = pl.multiple_of(group * (8 * LINES), 8)
        for k in range(8):
            asker = (step * groups + group) * 8 + k
            states = jnp.zeros((1, 128), f32)
            for s in range(SLOTS):
                entry = list_ref[asker, s]
                out_ref[pl.ds(start + k * LINES + 2 * s, 2), :] = table[
                    pl.ds(pl.multiple_of(2 * entry, 2), 2), :
                ]
                states = jnp.where(lane == s, state_ref[entry], states)
            out_ref[pl.ds(start + k * LINES + 2 * SLOTS, 1), :] = states
        return carry

    lax.fori_loop(0, groups, eight, 0)


def gather_rows(lists, states, own, minus, plus):
    devices = lists.shape[0]
    chunk = 32
    smem = pl.BlockSpec(memory_space=pltpu.SMEM)
    return pl.pallas_call(
        gather_kernel,
        grid=(devices // chunk,),
        in_specs=[smem, smem] + [pl.BlockSpec(memory_space=pl.ANY)] * 3,
        out_specs=pl.BlockSpec((chunk * LINES, 128), lambda i: (i, 0)),
        out_shape=jax.ShapeDtypeStruct((devices * LINES, 128), f32),
        scratch_shapes=[pltpu.VMEM((3 * own.shape[0], 128), f32), pltpu.SemaphoreType.DMA((3,))],
        compiler_params=pltpu.CompilerParams(vmem_limit_bytes=VMEM_LIMIT),
        cost_estimate=pl.CostEstimate(flops=0, bytes_accessed=8 * 10**6, transcendentals=0),
        name="gather_rows",
    )(lists, states, own, minus, plus)


def slots_kernel(
    start_ref, meta_ref, plan_ref, near_ref, own_ref, weight_ref, scale_ref, local_ref, high, low
):
    count = meta_ref.shape[1]
    rows, total = weight_ref.shape
    width = own_ref.shape[1]
    carrier = plan_ref[0:1, :]
    slot = plan_ref[1:2, :]
    four = jnp.floor(carrier * 0.25)
    pair = jnp.floor((carrier - 4.0 * four) * 0.5)
    odd = carrier - 4.0 * four - 2.0 * pair
    key = four * (2 * PAIR) + jnp.where(
        slot < FIRST,
        odd * 16 + pair * 8 + slot,
        32 + pair * 8 + odd * (8 - REST) + slot - FIRST,
    )
    key = jnp.where(slot < SLOTS, key, -1.0).astype(i32)
    reactant, product = meta_ref[0:1, :], meta_ref[1:2, :]
    param, constant = meta_ref[6:7, :], meta_ref[7:8, :]
    near = near_ref[8:9, :]
    scaled = constant * near
    a_high, a_low = split_int(reactant, 32.0)
    c_high, c_low = split_int(product, 32.0)
    line = iota((8, count), 0)
    packed = jnp.zeros((8, count), f32)
    for k, values in enumerate(
        (a_high, a_low, c_high, c_low, meta_ref[2:3, :], meta_ref[3:4, :])
    ):
        packed = jnp.where(line == k, values, packed)
    packed = packed.astype(bf16)
    high_part, low_part = halves(own_ref[...])
    high[...] = high_part
    low[...] = low_part
    block = 256
    for start in range(0, total, block):
        hot = iota((block, count), 0) + start == key
        found = nt(packed, jnp.where(hot, 1.0, 0.0).astype(bf16))
        a = (32.0 * found[0:1] + found[1:2]).astype(i32)
        c = (32.0 * found[2:3] + found[3:4]).astype(i32)
        species = iota((rows, block), 0)
        weight = jnp.where(species == c, found[5:6], 0.0) - jnp.where(
            species == a, found[4:5], 0.0
        )
        weight_ref[:, start : start + block] = weight.astype(bf16)

        def column(values):
            return jnp.sum(jnp.where(hot, values, 0.0), axis=1, keepdims=True)

        scale = column(scaled)
        scale_ref[start : start + block, :] = jnp.broadcast_to(scale, (block, 128))
        from_row = (iota((block, rows), 1) == column(reactant).astype(i32)).astype(bf16)
        chosen = iota((block, width), 1) + start_ref[0] == column(param).astype(i32)
        local_ref[start : start + block, :] = column(constant) * (
            nn(from_row, high[...]) + nn(from_row, low[...])
        ) + jnp.where(chosen, scale, 0.0)


def make_slots(start, meta, plan, near, own, devices):
    total = devices // 2 * PAIR
    rows, width = own.shape
    vmem = pl.BlockSpec(memory_space=pltpu.VMEM)
    return pl.pallas_call(
        slots_kernel,
        in_specs=[pl.BlockSpec(memory_space=pltpu.SMEM)] + [vmem] * 4,
        out_shape=(
            jax.ShapeDtypeStruct((rows, total), bf16),
            jax.ShapeDtypeStruct((total, 128), f32),
            jax.ShapeDtypeStruct((total, width), f32),
        ),
        scratch_shapes=[pltpu.VMEM((rows, width), bf16)] * 2,
        compiler_params=pltpu.CompilerParams(vmem_limit_bytes=VMEM_LIMIT),
        cost_estimate=pl.CostEstimate(flops=4 * 10**9, bytes_accessed=5 * 10**6, transcendentals=0),
        name="slots",
    )(start, meta, plan, near, own)


def near_kernel(meta_ref, state_ref, out_ref):
    count = meta_ref.shape[1]
    high, low = split_int(meta_ref[0:1, :], 128.0)
    low_hot = (iota((128, count), 0) == low.astype(i32)).astype(f32)
    columns = nn(state_ref[...], low_hot, lax.Precision.HIGHEST)
    picked = jnp.where(iota((8, count), 0) == high.astype(i32), columns, 0.0)
    out_ref[0:8, :] = picked
    out_ref[8:16, :] = jnp.broadcast_to(jnp.sum(picked, axis=0, keepdims=True), (8, count))


def near_state(meta, state):
    return pl.pallas_call(
        near_kernel,
        out_shape=jax.ShapeDtypeStruct((16, meta.shape[1]), f32),
        compiler_params=pltpu.CompilerParams(vmem_limit_bytes=VMEM_LIMIT),
        name="near_state",
    )(meta, state)


def band_kernel(
    columns_ref, counts_ref, own_ref, before_ref, after_ref, blocks_ref, out_ref, high, low
):
    step = pl.program_id(0)
    rows, width = own_ref.shape
    per_step, _, size, _ = blocks_ref.shape
    edge = before_ref.shape[0] // 2

    @pl.when(step == 0)
    def _():
        for half in range(2):
            columns = slice(half * 128, (half + 1) * 128)
            for values, at in (
                (before_ref[pl.ds(half, edge, stride=2), :], 0),
                (own_ref[:, columns], edge),
                (after_ref[pl.ds(half, edge, stride=2), :], edge + rows),
            ):
                high_part, low_part = halves(values)
                high[at : at + values.shape[0], columns] = high_part
                low[at : at + values.shape[0], columns] = low_part

    for r in range(per_step):
        place = step * per_step + r

        def add_slot(k, sum_so_far):
            at = pl.multiple_of(columns_ref[place, k] * size, size)
            block_high, block_low = halves(blocks_ref[r, k])
            rows_high = high[pl.ds(at, size), :]
            rows_low = low[pl.ds(at, size), :]
            return sum_so_far + (
                nn(block_high, rows_high) + (nn(block_low, rows_high) + nn(block_high, rows_low))
            )

        band = lax.fori_loop(0, counts_ref[place], add_slot, jnp.zeros((size, width), f32))
        at = pl.multiple_of(place * size, size)
        out_ref[r * size : (r + 1) * size, :] = own_ref[pl.ds(at, size), :] + step_length * band


def band_terms(columns, counts, own, before, after, blocks):
    rows, width = own.shape
    block_rows, slots, size, _ = blocks.shape
    per_step = 2
    edge = before.shape[0] // 2

    def whole(x):
        return pl.BlockSpec(x.shape, lambda i: (0,) * x.ndim)

    smem = pl.BlockSpec(memory_space=pltpu.SMEM)
    return pl.pallas_call(
        band_kernel,
        grid=(block_rows // per_step,),
        in_specs=[smem, smem]
        + [whole(x) for x in (own, before, after)]
        + [pl.BlockSpec((per_step, slots, size, size), lambda i: (i, 0, 0, 0))],
        out_specs=pl.BlockSpec((per_step * size, width), lambda i: (i, 0)),
        out_shape=jax.ShapeDtypeStruct((rows, width), f32),
        scratch_shapes=[pltpu.VMEM((rows + 2 * edge, width), bf16)] * 2,
        compiler_params=pltpu.CompilerParams(vmem_limit_bytes=VMEM_LIMIT),
        cost_estimate=pl.CostEstimate(
            flops=3 * 10**9, bytes_accessed=7 * 10**6, transcendentals=0
        ),
        name="band_terms",
    )(columns, counts, own, before, after, blocks)


def tail_kernel(
    far_hbm,
    scale_hbm,
    local_hbm,
    weight_hbm,
    base_hbm,
    out_hbm,
    far_ref,
    scale_ref,
    local_ref,
    weight_ref,
    base_ref,
    out_ref,
    high,
    low,
    sems,
    out_sems,
):
    lanes = far_ref.shape[1]
    rows, total = weight_ref.shape
    carriers = far_ref.shape[0] // LINES
    parts = 4
    block = rows // parts
    slices = ((far_hbm, far_ref), (scale_hbm, scale_ref), (local_hbm, local_ref))
    first = []
    for part in range(parts):
        copies = []
        for k, (source, target) in enumerate(slices):
            size = target.shape[0] // parts
            at = pl.ds(part * size, size)
            copies.append(pltpu.make_async_copy(source.at[at], target.at[at], sems.at[part, k]))
        first.append(copies)
    second = []
    for part in range(parts):
        at = pl.ds(part * block, block)
        second.append(
            [
                pltpu.make_async_copy(weight_hbm.at[at], weight_ref.at[at], sems.at[part, 3]),
                pltpu.make_async_copy(base_hbm.at[at], base_ref.at[at], sems.at[part, 4]),
            ]
        )
    for copies in first + second:
        for copy in copies:
            copy.start()

    lane, line = iota((8, lanes), 1), iota((8, lanes), 0)
    upper = line < REST

    def eight(group, carry):
        for k in range(2):
            values = [[[], []], [[], []], [[], []]]
            states = [[], [], []]
            for pair in range(2):
                at = pl.multiple_of(group * (8 * LINES), 8) + (4 * k + 2 * pair) * LINES
                following = at + LINES
                even_states = jnp.broadcast_to(far_ref[pl.ds(at + 2 * SLOTS, 1), :], (8, lanes))
                odd_states = jnp.broadcast_to(
                    far_ref[pl.ds(following + 2 * SLOTS, 1), :], (8, lanes)
                )
                states[0].append(jnp.where(lane == line, even_states, 0.0))
                states[1].append(jnp.where(lane == line, odd_states, 0.0))
                states[2].append(
                    jnp.where(
                        upper,
                        jnp.where(lane == line + FIRST, even_states, 0.0),
                        jnp.where(lane == line + SLOTS - 8, odd_states, 0.0),
                    )
                )
                for half in range(2):
                    values[0][half].append(far_ref[pl.ds(at + half, 8, stride=2), :])
                    values[1][half].append(far_ref[pl.ds(following + half, 8, stride=2), :])
                    values[2][half].append(
                        jnp.where(
                            upper,
                            far_ref[pl.ds(at + 2 * FIRST + half, 8, stride=2), :],
                            far_ref[pl.ds(following + 2 * (SLOTS - 8) + half, 8, stride=2), :],
                        )
                    )
            for j in range(3):
                state = jnp.sum(jnp.concatenate(states[j], axis=0), axis=1, keepdims=True)
                place = pl.ds(pl.multiple_of(group * (4 * PAIR), 16) + k * 2 * PAIR + j * 16, 16)
                for half in range(2):
                    columns = slice(half * lanes, (half + 1) * lanes)
                    mixed = (
                        jnp.concatenate(values[j][half], axis=0) * scale_ref[place, :]
                        + state * local_ref[place, columns]
                    )
                    high_part, low_part = halves(mixed)
                    high[place, columns] = high_part
                    low[place, columns] = low_part
        return carry

    groups = carriers // 8 // parts
    for part in range(parts):
        for copy in first[part]:
            copy.wait()
        lax.fori_loop(part * groups, (part + 1) * groups, eight, 0)

    stores = []
    for part in range(parts):
        for copy in second[part]:
            copy.wait()
        at = pl.ds(part * block, block)
        weight = weight_ref[at, :]
        sums = nn(weight, high[...]) + nn(weight, low[...])
        out_ref[at, :] = base_ref[at, :] + step_length * sums
        store = pltpu.make_async_copy(out_ref.at[at], out_hbm.at[at], out_sems.at[part])
        store.start()
        stores.append(store)
    for store in stores:
        store.wait()


def add_far(far, scale, local, weight, base):
    rows, total = weight.shape
    width = base.shape[1]
    held = [pltpu.VMEM(x.shape, x.dtype) for x in (far, scale, local, weight, base, base)]
    anywhere = pl.BlockSpec(memory_space=pl.ANY)
    return pl.pallas_call(
        tail_kernel,
        in_specs=[anywhere] * 5,
        out_specs=anywhere,
        out_shape=jax.ShapeDtypeStruct((rows, width), f32),
        scratch_shapes=held
        + [pltpu.VMEM((total, width), bf16)] * 2
        + [pltpu.SemaphoreType.DMA((4, 5)), pltpu.SemaphoreType.DMA((4,))],
        compiler_params=pltpu.CompilerParams(vmem_limit_bytes=VMEM_WHOLE),
        cost_estimate=pl.CostEstimate(
            flops=2 * 10**9, bytes_accessed=8 * 10**6, transcendentals=0
        ),
        name="add_far",
    )(far, scale, local, weight, base)


def exchange(x):
    return lax.all_to_all(x, "species", split_axis=0, concat_axis=0, tiled=True)


def add_overflow(result, start, meta, plan, near, direct, own, state):
    rows = exchange(own[direct])
    states = exchange(state[direct])
    owner = meta[4].astype(i32)
    rank = plan[2].astype(i32)
    reactant = meta[0].astype(i32)
    product = meta[1].astype(i32)
    constant = jnp.where(plan[1] == NONE, meta[7], 0.0)
    chosen = meta[6].astype(i32)[:, None] - start == iota((1, own.shape[1]), 1)
    growth = (constant * states[owner, rank])[:, None] * (
        own[reactant] + jnp.where(chosen, near[8][:, None], 0.0)
    ) + (constant * near[8])[:, None] * rows[owner, rank]
    result = result.at[product].add(step_length * meta[3][:, None] * growth)
    return result.at[reactant].add(-step_length * meta[2][:, None] * growth)


def body(
    species_state,
    sensitivity,
    jacobian_blocks,
    block_columns,
    block_counts,
    reaction_rows,
    stoichiometry,
    catalyst_device,
    catalyst_row,
    param_index,
    rate_constant,
):
    devices = lax.axis_size("species")
    rows, width = sensitivity.shape
    block_rows, _, size, _ = jacobian_blocks.shape
    edge = H * size
    ends = devices - 1

    place = lax.axis_index("species")
    first, last = place % STRIDE == 0, place % STRIDE == STRIDE - 1
    state_table = species_state.reshape(-1, 128)
    local_meta = pack(
        reaction_rows, stoichiometry, catalyst_device, catalyst_row, param_index, rate_constant
    )
    other_meta = lax.ppermute(local_meta, "params", [(0, 1), (1, 0)])
    own, _ = lax.optimization_barrier((sensitivity, local_meta))
    table = make_table(own, state_table)
    onward = [(i, (i + STRIDE) % devices) for i in range(devices)]
    minus = lax.ppermute(table, "species", onward)
    plus = lax.ppermute(table, "species", [(b, a) for a, b in onward])

    request, plan, meta = make_plan(local_meta, other_meta, devices)
    asked = exchange(request)
    lists = asked[:, :SLOTS].astype(i32)
    padding = jnp.zeros((SPAN - rows,), f32)
    states = jnp.concatenate(
        [
            piece
            for lines in (state_table, minus[2 * rows :], plus[2 * rows :])
            for piece in (lines.reshape(-1), padding)
        ]
    )
    message = gather_rows(lists, states, table, minus, plus)
    far = exchange(message.reshape(devices, 1, LINES * 128)).reshape(-1, 128)

    own, lines, minus, plus, _ = lax.optimization_barrier(
        (sensitivity, table, minus, plus, message)
    )
    tail = slice(2 * (rows - edge), 2 * rows)
    head = slice(0, 2 * edge)
    onward = [(i, i // STRIDE * STRIDE + (i + 1) % STRIDE) for i in range(devices)]
    before = lax.ppermute(jnp.where(last, minus[tail], lines[tail]), "species", onward)
    after = lax.ppermute(
        jnp.where(first, plus[head], lines[head]), "species", [(b, a) for a, b in onward]
    )
    columns = block_columns - lax.axis_index("species") * block_rows + H
    near = near_state(meta, state_table)
    start = (lax.axis_index("params") * width).astype(i32).reshape(1)
    weight, scale, local = make_slots(start, meta, plan, near, own, devices)
    base = band_terms(columns, block_counts, own, before, after, jacobian_blocks)
    result = add_far(far, scale, local, weight, base)
    direct = asked[:, DIRECT : DIRECT + RANKS].astype(i32)
    return lax.cond(
        jnp.any(asked[:, FLAG] > 0),
        lambda x: add_overflow(
            x, start, meta, plan, near, direct, sensitivity, species_state
        ),
        lambda x: x,
        result,
    )


def solution(mesh):
    specs = (
        P("species"),
        P("species", "params"),
        P("species", None, None, None),
        P("species", None),
        P("species"),
        P(("species", "params"), None),
        P(("species", "params"), None),
        P(("species", "params"), None),
        P(("species", "params")),
        P(("species", "params")),
        P(("species", "params")),
    )
    return jax.shard_map(
        body, mesh=mesh, in_specs=specs, out_specs=P("species", "params"), check_vma=False
    )
```

```python
import functools

import jax
import jax.numpy as jnp
from jax import lax
from jax.experimental import pallas as pl
from jax.experimental.pallas import tpu as pltpu
from jax.sharding import PartitionSpec as P

H = 3
CHAIN = 32
STRIDE = 4
SLOTS = 11
FIRST = 8
REST = SLOTS - FIRST
PAIR = 24
LINES = 2 * SLOTS + 1
SPAN = 1028
RANKS = 16
DIRECT = 16
FLAG = 32
NONE = 127
VMEM_LIMIT = 24 * 1024 * 1024
VMEM_WHOLE = 60 * 1024 * 1024

step_length = 0.5
f32 = jnp.float32
bf16 = jnp.bfloat16
i32 = jnp.int32
f8 = jnp.float8_e4m3fn
LOW_SCALE = 4096.0


def nt(a, b):
    return lax.dot_general(a, b, (((1,), (1,)), ((), ())), preferred_element_type=f32)


def nn(a, b, precision=None):
    return jnp.dot(a, b, preferred_element_type=f32, precision=precision)


def iota(shape, dim):
    return lax.broadcasted_iota(i32, shape, dim)


def halves(x):
    high = x.astype(bf16)
    return high, (x - high.astype(f32)).astype(bf16)


def split_int(x, base):
    high = jnp.floor(x * (1.0 / base))
    return high, x - base * high


def placed(device):
    return (device % STRIDE) * CHAIN + device // STRIDE


def pack_kernel(rows_ref, amounts_ref, owner_ref, row_ref, param_ref, constant_ref, out_ref):
    out_ref[0:2, :] = rows_ref[...].astype(f32)
    out_ref[2:4, :] = amounts_ref[...].astype(f32)
    out_ref[4:5, :] = owner_ref[...].astype(f32)
    out_ref[5:6, :] = row_ref[...].astype(f32)
    out_ref[6:7, :] = param_ref[...].astype(f32)
    out_ref[7:8, :] = constant_ref[...]


def pack(rows_pair, stoichiometry, owner, row, param, constant):
    count = constant.shape[0]
    return pl.pallas_call(
        pack_kernel,
        out_shape=jax.ShapeDtypeStruct((8, count), f32),
        name="pack",
    )(
        rows_pair.T,
        stoichiometry.T,
        owner.T,
        row.reshape(1, count),
        param.reshape(1, count),
        constant.reshape(1, count),
    )


def table_kernel(own_ref, state_ref, out_ref):
    rows, width = own_ref.shape
    for half in range(2):
        out_ref[pl.ds(half, rows, stride=2), :] = own_ref[:, half * 128 : half * 128 + 128]
    out_ref[2 * rows :, :] = state_ref[...]


def make_table(own, state):
    rows = own.shape[0]
    return pl.pallas_call(
        table_kernel,
        out_shape=jax.ShapeDtypeStruct((2 * rows + state.shape[0], 128), f32),
        compiler_params=pltpu.CompilerParams(vmem_limit_bytes=VMEM_LIMIT),
        name="table",
    )(own, state)


def plan_kernel(local_ref, other_ref, request_ref, plan_ref, meta_ref):
    count = meta_ref.shape[1]
    devices = request_ref.shape[0]
    meta_ref[:, : count // 2] = local_ref[...]
    meta_ref[:, count // 2 :] = other_ref[...]
    owner = meta_ref[4:5, :]
    row = meta_ref[5:6, :]
    owner_hot = (iota((devices, count), 0) == owner.astype(i32)).astype(bf16)
    before = (iota((count, count), 0) < iota((count, count), 1)).astype(bf16)
    earlier = nn(owner_hot, before)
    rank = jnp.sum(earlier * owner_hot.astype(f32), axis=0, keepdims=True)
    load = nt(jnp.ones((8, count), bf16), owner_hot)

    spread = (CHAIN * 8, devices)
    held = jnp.where(
        iota(spread, 1) // STRIDE == iota(spread, 0) // 8, load[0:1, :], 0.0
    )
    square = (devices, 128)
    loads = nn(
        held.astype(bf16), (iota(square, 0) % STRIDE == iota(square, 1)).astype(bf16)
    )
    zero = jnp.zeros((8, 128), f32)
    room = f32(SLOTS)
    late, own, ahead = [], [], [zero]
    left = zero
    for z in range(CHAIN):
        here = loads[8 * z : 8 * z + 8]
        late.append(jnp.minimum(left, room))
        mine = here - ahead[z]
        own.append(jnp.minimum(mine, room - late[z]))
        left = mine - own[z]
        if z + 1 < CHAIN:
            ahead.append(
                jnp.minimum(loads[8 * z + 8 : 8 * z + 16], room - late[z] - own[z])
            )
    late.append(zero)
    end_own = [ahead[z] + own[z] for z in range(CHAIN)]
    end_late = [end_own[z] + late[z + 1] for z in range(CHAIN)]
    start_ahead = [zero] + [late[z] + own[z] for z in range(CHAIN - 1)]
    missed = zero
    for z in range(CHAIN):
        missed = missed + (loads[8 * z : 8 * z + 8] - end_late[z])
    overflow = jnp.sum(missed, axis=1, keepdims=True)

    line = iota((8, 128), 0)
    tiles = []
    for values in (ahead, end_own, end_late, start_ahead, late):
        for start in range(0, CHAIN, 8):
            tile = values[start]
            for k in range(1, 8):
                tile = jnp.where(line == k, values[start + k], tile)
            tiles.append(tile)
    place = placed(owner.astype(i32))
    chain_hot = (iota((128, count), 0) == place // CHAIN).astype(bf16)
    looked = nn(jnp.concatenate(tiles, axis=0).astype(bf16), chain_hot)
    at_place = iota((CHAIN, count), 0) == place % CHAIN
    ahead_q, end_own_q, end_late_q, start_ahead_q, late_q = [
        jnp.sum(
            jnp.where(at_place, looked[k * CHAIN : (k + 1) * CHAIN], 0.0), axis=0, keepdims=True
        )
        for k in range(5)
    ]
    is_ahead = rank < ahead_q
    is_own = rank < end_own_q
    is_late = rank < end_late_q
    slot = jnp.where(
        is_ahead,
        start_ahead_q + rank,
        jnp.where(
            is_own,
            late_q + rank - ahead_q,
            jnp.where(is_late, rank - end_own_q, f32(NONE)),
        ),
    )
    shift = jnp.where(is_ahead, -1.0, jnp.where(is_own, 0.0, jnp.where(is_late, 1.0, 0.0)))
    part = jnp.where(is_ahead, 2.0, jnp.where(is_own, 0.0, jnp.where(is_late, 1.0, 0.0)))
    carrier = owner + STRIDE * shift
    entry = part * f32(SPAN) + row
    carrier_hot = (iota((devices, count), 0) == carrier.astype(i32)).astype(bf16)
    slot_line = iota((128, count), 0)
    slot_hot = jnp.logical_and(slot_line == slot.astype(i32), slot_line < SLOTS)
    rank_hot = slot_line == rank.astype(i32) + DIRECT
    entry_high, entry_low = split_int(entry, 64.0)
    row_high, row_low = split_int(row, 64.0)

    def listed(hot, places, values):
        return nt(hot, jnp.where(places, values, 0.0).astype(bf16))

    request = 64.0 * (
        listed(carrier_hot, slot_hot, entry_high) + listed(owner_hot, rank_hot, row_high)
    )
    request = request + (
        listed(carrier_hot, slot_hot, entry_low) + listed(owner_hot, rank_hot, row_low)
    )
    lane_out = iota((devices, 128), 1)
    request_ref[...] = jnp.where(lane_out == FLAG, overflow[0:1, 0:1], request)
    line_out = iota((8, count), 0)
    plan = jnp.zeros((8, count), f32)
    for k, values in enumerate((carrier, slot, rank)):
        plan = jnp.where(line_out == k, values, plan)
    plan_ref[...] = plan


def make_plan(local, other, devices):
    count = 2 * local.shape[1]
    return pl.pallas_call(
        plan_kernel,
        out_shape=(
            jax.ShapeDtypeStruct((devices, 128), f32),
            jax.ShapeDtypeStruct((8, count), f32),
            jax.ShapeDtypeStruct((8, count), f32),
        ),
        compiler_params=pltpu.CompilerParams(vmem_limit_bytes=VMEM_LIMIT),
        cost_estimate=pl.CostEstimate(flops=10**9, bytes_accessed=200000, transcendentals=0),
        name="plan",
    )(local, other)


def gather_kernel(list_ref, state_ref, own_ref, minus_ref, plus_ref, out_ref, table, sems):
    step = pl.program_id(0)
    lines = own_ref.shape[0]
    groups = out_ref.shape[0] // (8 * LINES)

    @pl.when(step == 0)
    def _():
        copies = [
            pltpu.make_async_copy(part, table.at[pl.ds(k * lines, lines)], sems.at[k])
            for k, part in enumerate((own_ref, minus_ref, plus_ref))
        ]
        for copy in copies:
            copy.start()
        for copy in copies:
            copy.wait()

    lane = iota((1, 128), 1)

    def eight(group, carry):
        start = pl.multiple_of(group * (8 * LINES), 8)
        for k in range(8):
            asker = (step * groups + group) * 8 + k
            states = jnp.zeros((1, 128), f32)
            for s in range(SLOTS):
                entry = list_ref[asker, s]
                out_ref[pl.ds(start + k * LINES + 2 * s, 2), :] = table[
                    pl.ds(pl.multiple_of(2 * entry, 2), 2), :
                ]
                states = jnp.where(lane == s, state_ref[entry], states)
            out_ref[pl.ds(start + k * LINES + 2 * SLOTS, 1), :] = states
        return carry

    lax.fori_loop(0, groups, eight, 0)


def gather_rows(lists, states, own, minus, plus):
    devices = lists.shape[0]
    chunk = 32
    smem = pl.BlockSpec(memory_space=pltpu.SMEM)
    return pl.pallas_call(
        gather_kernel,
        grid=(devices // chunk,),
        in_specs=[smem, smem] + [pl.BlockSpec(memory_space=pl.ANY)] * 3,
        out_specs=pl.BlockSpec((chunk * LINES, 128), lambda i: (i, 0)),
        out_shape=jax.ShapeDtypeStruct((devices * LINES, 128), f32),
        scratch_shapes=[pltpu.VMEM((3 * own.shape[0], 128), f32), pltpu.SemaphoreType.DMA((3,))],
        compiler_params=pltpu.CompilerParams(vmem_limit_bytes=VMEM_LIMIT),
        cost_estimate=pl.CostEstimate(flops=0, bytes_accessed=8 * 10**6, transcendentals=0),
        name="gather_rows",
    )(lists, states, own, minus, plus)


def slots_kernel(
    start_ref, meta_ref, plan_ref, near_ref, own_ref, weight_ref, scale_ref, local_ref, high, low
):
    count = meta_ref.shape[1]
    rows, total = weight_ref.shape
    width = own_ref.shape[1]
    carrier = plan_ref[0:1, :]
    slot = plan_ref[1:2, :]
    four = jnp.floor(carrier * 0.25)
    pair = jnp.floor((carrier - 4.0 * four) * 0.5)
    odd = carrier - 4.0 * four - 2.0 * pair
    key = four * (2 * PAIR) + jnp.where(
        slot < FIRST,
        odd * 16 + pair * 8 + slot,
        32 + pair * 8 + odd * (8 - REST) + slot - FIRST,
    )
    key = jnp.where(slot < SLOTS, key, -1.0).astype(i32)
    reactant, product = meta_ref[0:1, :], meta_ref[1:2, :]
    param, constant = meta_ref[6:7, :], meta_ref[7:8, :]
    near = near_ref[8:9, :]
    scaled = constant * near
    a_high, a_low = split_int(reactant, 32.0)
    c_high, c_low = split_int(product, 32.0)
    line = iota((8, count), 0)
    packed = jnp.zeros((8, count), f32)
    for k, values in enumerate(
        (a_high, a_low, c_high, c_low, meta_ref[2:3, :], meta_ref[3:4, :])
    ):
        packed = jnp.where(line == k, values, packed)
    packed = packed.astype(bf16)
    high_part, low_part = halves(own_ref[...])
    high[...] = high_part
    low[...] = low_part
    block = 256
    for start in range(0, total, block):
        hot = iota((block, count), 0) + start == key
        found = nt(packed, jnp.where(hot, 1.0, 0.0).astype(bf16))
        a = (32.0 * found[0:1] + found[1:2]).astype(i32)
        c = (32.0 * found[2:3] + found[3:4]).astype(i32)
        species = iota((rows, block), 0)
        weight = jnp.where(species == c, found[5:6], 0.0) - jnp.where(
            species == a, found[4:5], 0.0
        )
        weight_ref[:, start : start + block] = weight.astype(f8)

        def column(values):
            return jnp.sum(jnp.where(hot, values, 0.0), axis=1, keepdims=True)

        scale = column(scaled)
        scale_ref[start : start + block, :] = jnp.broadcast_to(scale, (block, 128))
        from_row = (iota((block, rows), 1) == column(reactant).astype(i32)).astype(bf16)
        chosen = iota((block, width), 1) + start_ref[0] == column(param).astype(i32)
        local_ref[start : start + block, :] = column(constant) * (
            nn(from_row, high[...]) + nn(from_row, low[...])
        ) + jnp.where(chosen, scale, 0.0)


def make_slots(start, meta, plan, near, own, devices):
    total = devices // 2 * PAIR
    rows, width = own.shape
    vmem = pl.BlockSpec(memory_space=pltpu.VMEM)
    return pl.pallas_call(
        slots_kernel,
        in_specs=[pl.BlockSpec(memory_space=pltpu.SMEM)] + [vmem] * 4,
        out_shape=(
            jax.ShapeDtypeStruct((rows, total), f8),
            jax.ShapeDtypeStruct((total, 128), f32),
            jax.ShapeDtypeStruct((total, width), f32),
        ),
        scratch_shapes=[pltpu.VMEM((rows, width), bf16)] * 2,
        compiler_params=pltpu.CompilerParams(vmem_limit_bytes=VMEM_LIMIT),
        cost_estimate=pl.CostEstimate(flops=4 * 10**9, bytes_accessed=5 * 10**6, transcendentals=0),
        name="slots",
    )(start, meta, plan, near, own)


def near_kernel(meta_ref, state_ref, out_ref):
    count = meta_ref.shape[1]
    high, low = split_int(meta_ref[0:1, :], 128.0)
    low_hot = (iota((128, count), 0) == low.astype(i32)).astype(f32)
    columns = nn(state_ref[...], low_hot, lax.Precision.HIGHEST)
    picked = jnp.where(iota((8, count), 0) == high.astype(i32), columns, 0.0)
    out_ref[0:8, :] = picked
    out_ref[8:16, :] = jnp.broadcast_to(jnp.sum(picked, axis=0, keepdims=True), (8, count))


def near_state(meta, state):
    return pl.pallas_call(
        near_kernel,
        out_shape=jax.ShapeDtypeStruct((16, meta.shape[1]), f32),
        compiler_params=pltpu.CompilerParams(vmem_limit_bytes=VMEM_LIMIT),
        name="near_state",
    )(meta, state)


def band_kernel(
    columns_ref, counts_ref, own_ref, before_ref, after_ref, blocks_ref, out_ref, high, low
):
    step = pl.program_id(0)
    rows, width = own_ref.shape
    per_step, _, size, _ = blocks_ref.shape
    edge = before_ref.shape[0] // 2

    @pl.when(step == 0)
    def _():
        for half in range(2):
            columns = slice(half * 128, (half + 1) * 128)
            for values, at in (
                (before_ref[pl.ds(half, edge, stride=2), :], 0),
                (own_ref[:, columns], edge),
                (after_ref[pl.ds(half, edge, stride=2), :], edge + rows),
            ):
                high_part, low_part = halves(values)
                high[at : at + values.shape[0], columns] = high_part
                low[at : at + values.shape[0], columns] = low_part

    for r in range(per_step):
        place = step * per_step + r

        def add_slot(k, sum_so_far):
            at = pl.multiple_of(columns_ref[place, k] * size, size)
            block_high, block_low = halves(blocks_ref[r, k])
            rows_high = high[pl.ds(at, size), :]
            rows_low = low[pl.ds(at, size), :]
            return sum_so_far + (
                nn(block_high, rows_high) + (nn(block_low, rows_high) + nn(block_high, rows_low))
            )

        band = lax.fori_loop(0, counts_ref[place], add_slot, jnp.zeros((size, width), f32))
        at = pl.multiple_of(place * size, size)
        out_ref[r * size : (r + 1) * size, :] = own_ref[pl.ds(at, size), :] + step_length * band


def band_terms(columns, counts, own, before, after, blocks):
    rows, width = own.shape
    block_rows, slots, size, _ = blocks.shape
    per_step = 2
    edge = before.shape[0] // 2

    def whole(x):
        return pl.BlockSpec(x.shape, lambda i: (0,) * x.ndim)

    smem = pl.BlockSpec(memory_space=pltpu.SMEM)
    return pl.pallas_call(
        band_kernel,
        grid=(block_rows // per_step,),
        in_specs=[smem, smem]
        + [whole(x) for x in (own, before, after)]
        + [pl.BlockSpec((per_step, slots, size, size), lambda i: (i, 0, 0, 0))],
        out_specs=pl.BlockSpec((per_step * size, width), lambda i: (i, 0)),
        out_shape=jax.ShapeDtypeStruct((rows, width), f32),
        scratch_shapes=[pltpu.VMEM((rows + 2 * edge, width), bf16)] * 2,
        compiler_params=pltpu.CompilerParams(vmem_limit_bytes=VMEM_LIMIT),
        cost_estimate=pl.CostEstimate(
            flops=3 * 10**9, bytes_accessed=7 * 10**6, transcendentals=0
        ),
        name="band_terms",
    )(columns, counts, own, before, after, blocks)


def tail_kernel(
    far_hbm,
    scale_hbm,
    local_hbm,
    weight_hbm,
    base_hbm,
    out_hbm,
    far_ref,
    scale_ref,
    local_ref,
    weight_ref,
    base_ref,
    out_ref,
    high,
    low,
    low_small,
    sems,
    out_sems,
):
    lanes = far_ref.shape[1]
    rows, total = weight_ref.shape
    carriers = far_ref.shape[0] // LINES
    parts = 4
    block = rows // parts
    slices = ((far_hbm, far_ref), (scale_hbm, scale_ref), (local_hbm, local_ref))
    first = []
    for part in range(parts):
        copies = []
        for k, (source, target) in enumerate(slices):
            size = target.shape[0] // parts
            at = pl.ds(part * size, size)
            copies.append(pltpu.make_async_copy(source.at[at], target.at[at], sems.at[part, k]))
        first.append(copies)
    second = []
    for part in range(parts):
        at = pl.ds(part * block, block)
        second.append(
            [
                pltpu.make_async_copy(weight_hbm.at[at], weight_ref.at[at], sems.at[part, 3]),
                pltpu.make_async_copy(base_hbm.at[at], base_ref.at[at], sems.at[part, 4]),
            ]
        )
    for copies in first + second:
        for copy in copies:
            copy.start()

    lane, line = iota((8, lanes), 1), iota((8, lanes), 0)
    upper = line < REST

    def eight(group, carry):
        for k in range(2):
            values = [[[], []], [[], []], [[], []]]
            states = [[], [], []]
            for pair in range(2):
                at = pl.multiple_of(group * (8 * LINES), 8) + (4 * k + 2 * pair) * LINES
                following = at + LINES
                even_states = jnp.broadcast_to(far_ref[pl.ds(at + 2 * SLOTS, 1), :], (8, lanes))
                odd_states = jnp.broadcast_to(
                    far_ref[pl.ds(following + 2 * SLOTS, 1), :], (8, lanes)
                )
                states[0].append(jnp.where(lane == line, even_states, 0.0))
                states[1].append(jnp.where(lane == line, odd_states, 0.0))
                states[2].append(
                    jnp.where(
                        upper,
                        jnp.where(lane == line + FIRST, even_states, 0.0),
                        jnp.where(lane == line + SLOTS - 8, odd_states, 0.0),
                    )
                )
                for half in range(2):
                    values[0][half].append(far_ref[pl.ds(at + half, 8, stride=2), :])
                    values[1][half].append(far_ref[pl.ds(following + half, 8, stride=2), :])
                    values[2][half].append(
                        jnp.where(
                            upper,
                            far_ref[pl.ds(at + 2 * FIRST + half, 8, stride=2), :],
                            far_ref[pl.ds(following + 2 * (SLOTS - 8) + half, 8, stride=2), :],
                        )
                    )
            for j in range(3):
                state = jnp.sum(jnp.concatenate(states[j], axis=0), axis=1, keepdims=True)
                place = pl.ds(pl.multiple_of(group * (4 * PAIR), 16) + k * 2 * PAIR + j * 16, 16)
                for half in range(2):
                    columns = slice(half * lanes, (half + 1) * lanes)
                    mixed = (
                        jnp.concatenate(values[j][half], axis=0) * scale_ref[place, :]
                        + state * local_ref[place, columns]
                    )
                    high_part = mixed.astype(bf16)
                    low_part = (mixed - high_part.astype(f32)) * LOW_SCALE
                    high[place, columns] = high_part
                    low[place, columns] = low_part.astype(bf16)
        return carry

    groups = carriers // 8 // parts
    for part in range(parts):
        for copy in first[part]:
            copy.wait()
        lax.fori_loop(part * groups, (part + 1) * groups, eight, 0)

    low_small[...] = low[...].astype(f8)
    stores = []
    for part in range(parts):
        for copy in second[part]:
            copy.wait()
        at = pl.ds(part * block, block)
        weight = weight_ref[at, :]
        sums = nn(weight.astype(bf16), high[...])
        sums = sums + nn(weight, low_small[...]) * (1.0 / LOW_SCALE)
        out_ref[at, :] = base_ref[at, :] + step_length * sums
        store = pltpu.make_async_copy(out_ref.at[at], out_hbm.at[at], out_sems.at[part])
        store.start()
        stores.append(store)
    for store in stores:
        store.wait()


def add_far(far, scale, local, weight, base):
    rows, total = weight.shape
    width = base.shape[1]
    held = [pltpu.VMEM(x.shape, x.dtype) for x in (far, scale, local, weight, base, base)]
    anywhere = pl.BlockSpec(memory_space=pl.ANY)
    return pl.pallas_call(
        tail_kernel,
        in_specs=[anywhere] * 5,
        out_specs=anywhere,
        out_shape=jax.ShapeDtypeStruct((rows, width), f32),
        scratch_shapes=held
        + [pltpu.VMEM((total, width), bf16)] * 2
        + [pltpu.VMEM((total, width), f8)]
        + [pltpu.SemaphoreType.DMA((4, 5)), pltpu.SemaphoreType.DMA((4,))],
        compiler_params=pltpu.CompilerParams(vmem_limit_bytes=VMEM_WHOLE),
        cost_estimate=pl.CostEstimate(
            flops=2 * 10**9, bytes_accessed=8 * 10**6, transcendentals=0
        ),
        name="add_far",
    )(far, scale, local, weight, base)


def exchange(x):
    return lax.all_to_all(x, "species", split_axis=0, concat_axis=0, tiled=True)


def add_overflow(result, start, meta, plan, near, direct, own, state):
    rows = exchange(own[direct])
    states = exchange(state[direct])
    owner = meta[4].astype(i32)
    rank = plan[2].astype(i32)
    reactant = meta[0].astype(i32)
    product = meta[1].astype(i32)
    constant = jnp.where(plan[1] == NONE, meta[7], 0.0)
    chosen = meta[6].astype(i32)[:, None] - start == iota((1, own.shape[1]), 1)
    growth = (constant * states[owner, rank])[:, None] * (
        own[reactant] + jnp.where(chosen, near[8][:, None], 0.0)
    ) + (constant * near[8])[:, None] * rows[owner, rank]
    result = result.at[product].add(step_length * meta[3][:, None] * growth)
    return result.at[reactant].add(-step_length * meta[2][:, None] * growth)


def body(
    species_state,
    sensitivity,
    jacobian_blocks,
    block_columns,
    block_counts,
    reaction_rows,
    stoichiometry,
    catalyst_device,
    catalyst_row,
    param_index,
    rate_constant,
):
    devices = lax.axis_size("species")
    rows, width = sensitivity.shape
    block_rows, _, size, _ = jacobian_blocks.shape
    edge = H * size
    ends = devices - 1

    place = lax.axis_index("species")
    first, last = place % STRIDE == 0, place % STRIDE == STRIDE - 1
    state_table = species_state.reshape(-1, 128)
    local_meta = pack(
        reaction_rows, stoichiometry, catalyst_device, catalyst_row, param_index, rate_constant
    )
    other_meta = lax.ppermute(local_meta, "params", [(0, 1), (1, 0)])
    own, _ = lax.optimization_barrier((sensitivity, local_meta))
    table = make_table(own, state_table)
    onward = [(i, (i + STRIDE) % devices) for i in range(devices)]
    minus = lax.ppermute(table, "species", onward)
    plus = lax.ppermute(table, "species", [(b, a) for a, b in onward])

    request, plan, meta = make_plan(local_meta, other_meta, devices)
    asked = exchange(request)
    lists = asked[:, :SLOTS].astype(i32)
    padding = jnp.zeros((SPAN - rows,), f32)
    states = jnp.concatenate(
        [
            piece
            for lines in (state_table, minus[2 * rows :], plus[2 * rows :])
            for piece in (lines.reshape(-1), padding)
        ]
    )
    message = gather_rows(lists, states, table, minus, plus)
    far = exchange(message.reshape(devices, 1, LINES * 128)).reshape(-1, 128)

    own, lines, minus, plus, _ = lax.optimization_barrier(
        (sensitivity, table, minus, plus, message)
    )
    tail = slice(2 * (rows - edge), 2 * rows)
    head = slice(0, 2 * edge)
    onward = [(i, i // STRIDE * STRIDE + (i + 1) % STRIDE) for i in range(devices)]
    before = lax.ppermute(jnp.where(last, minus[tail], lines[tail]), "species", onward)
    after = lax.ppermute(
        jnp.where(first, plus[head], lines[head]), "species", [(b, a) for a, b in onward]
    )
    columns = block_columns - lax.axis_index("species") * block_rows + H
    near = near_state(meta, state_table)
    start = (lax.axis_index("params") * width).astype(i32).reshape(1)
    weight, scale, local = make_slots(start, meta, plan, near, own, devices)
    base = band_terms(columns, block_counts, own, before, after, jacobian_blocks)
    result = add_far(far, scale, local, weight, base)
    direct = asked[:, DIRECT : DIRECT + RANKS].astype(i32)
    return lax.cond(
        jnp.any(asked[:, FLAG] > 0),
        lambda x: add_overflow(
            x, start, meta, plan, near, direct, sensitivity, species_state
        ),
        lambda x: x,
        result,
    )


def solution(mesh):
    specs = (
        P("species"),
        P("species", "params"),
        P("species", None, None, None),
        P("species", None),
        P("species"),
        P(("species", "params"), None),
        P(("species", "params"), None),
        P(("species", "params"), None),
        P(("species", "params")),
        P(("species", "params")),
        P(("species", "params")),
    )
    return jax.shard_map(
        body, mesh=mesh, in_specs=specs, out_specs=P("species", "params"), check_vma=False
    )
```

```python
import functools

import jax
import jax.numpy as jnp
from jax import lax
from jax.experimental import pallas as pl
from jax.experimental.pallas import tpu as pltpu
from jax.sharding import PartitionSpec as P

H = 3
CHAIN = 32
STRIDE = 4
SLOTS = 11
FIRST = 8
REST = SLOTS - FIRST
PAIR = 24
LINES = 2 * SLOTS + 1
SPAN = 1028
RANKS = 16
DIRECT = 16
FLAG = 32
NONE = 127
VMEM_LIMIT = 24 * 1024 * 1024
VMEM_WHOLE = 60 * 1024 * 1024

step_length = 0.5
f32 = jnp.float32
bf16 = jnp.bfloat16
i32 = jnp.int32
f8 = jnp.float8_e4m3fn
LOW_SCALE = 4096.0


def nt(a, b):
    return lax.dot_general(a, b, (((1,), (1,)), ((), ())), preferred_element_type=f32)


def nn(a, b, precision=None):
    return jnp.dot(a, b, preferred_element_type=f32, precision=precision)


def iota(shape, dim):
    return lax.broadcasted_iota(i32, shape, dim)


def halves(x):
    high = x.astype(bf16)
    return high, (x - high.astype(f32)).astype(bf16)


def split_int(x, base):
    high = jnp.floor(x * (1.0 / base))
    return high, x - base * high


def placed(device):
    return (device % STRIDE) * CHAIN + device // STRIDE


def prepare_kernel(
    rows_ref,
    amounts_ref,
    owner_ref,
    row_ref,
    param_ref,
    constant_ref,
    own_ref,
    state_ref,
    meta_ref,
    table_ref,
):
    meta_ref[0:2, :] = rows_ref[...].astype(f32)
    meta_ref[2:4, :] = amounts_ref[...].astype(f32)
    meta_ref[4:5, :] = owner_ref[...].astype(f32)
    meta_ref[5:6, :] = row_ref[...].astype(f32)
    meta_ref[6:7, :] = param_ref[...].astype(f32)
    meta_ref[7:8, :] = constant_ref[...]
    rows = own_ref.shape[0]
    for half in range(2):
        table_ref[pl.ds(half, rows, stride=2), :] = own_ref[:, half * 128 : half * 128 + 128]
    table_ref[2 * rows :, :] = state_ref[...]


def prepare(rows_pair, stoichiometry, owner, row, param, constant, own, state):
    count = constant.shape[0]
    rows = own.shape[0]
    return pl.pallas_call(
        prepare_kernel,
        out_shape=(
            jax.ShapeDtypeStruct((8, count), f32),
            jax.ShapeDtypeStruct((2 * rows + state.shape[0], 128), f32),
        ),
        name="prepare",
    )(
        rows_pair.T,
        stoichiometry.T,
        owner.T,
        row.reshape(1, count),
        param.reshape(1, count),
        constant.reshape(1, count),
        own,
        state,
    )


def plan_kernel(local_ref, other_ref, request_ref, plan_ref, meta_ref):
    count = meta_ref.shape[1]
    devices = request_ref.shape[0]
    meta_ref[:, : count // 2] = local_ref[...]
    meta_ref[:, count // 2 :] = other_ref[...]
    owner = meta_ref[4:5, :]
    row = meta_ref[5:6, :]
    owner_hot = (iota((devices, count), 0) == owner.astype(i32)).astype(bf16)
    before = (iota((count, count), 0) < iota((count, count), 1)).astype(bf16)
    earlier = nn(owner_hot, before)
    rank = jnp.sum(earlier * owner_hot.astype(f32), axis=0, keepdims=True)
    load = nt(jnp.ones((8, count), bf16), owner_hot)

    spread = (CHAIN * 8, devices)
    held = jnp.where(
        iota(spread, 1) // STRIDE == iota(spread, 0) // 8, load[0:1, :], 0.0
    )
    square = (devices, 128)
    loads = nn(
        held.astype(bf16), (iota(square, 0) % STRIDE == iota(square, 1)).astype(bf16)
    )
    zero = jnp.zeros((8, 128), f32)
    room = f32(SLOTS)
    late, own, ahead = [], [], [zero]
    left = zero
    for z in range(CHAIN):
        here = loads[8 * z : 8 * z + 8]
        late.append(jnp.minimum(left, room))
        mine = here - ahead[z]
        own.append(jnp.minimum(mine, room - late[z]))
        left = mine - own[z]
        if z + 1 < CHAIN:
            ahead.append(
                jnp.minimum(loads[8 * z + 8 : 8 * z + 16], room - late[z] - own[z])
            )
    late.append(zero)
    end_own = [ahead[z] + own[z] for z in range(CHAIN)]
    end_late = [end_own[z] + late[z + 1] for z in range(CHAIN)]
    start_ahead = [zero] + [late[z] + own[z] for z in range(CHAIN - 1)]
    missed = zero
    for z in range(CHAIN):
        missed = missed + (loads[8 * z : 8 * z + 8] - end_late[z])
    overflow = jnp.sum(missed, axis=1, keepdims=True)

    line = iota((8, 128), 0)
    tiles = []
    for values in (ahead, end_own, end_late, start_ahead, late):
        for start in range(0, CHAIN, 8):
            tile = values[start]
            for k in range(1, 8):
                tile = jnp.where(line == k, values[start + k], tile)
            tiles.append(tile)
    place = placed(owner.astype(i32))
    chain_hot = (iota((128, count), 0) == place // CHAIN).astype(bf16)
    looked = nn(jnp.concatenate(tiles, axis=0).astype(bf16), chain_hot)
    at_place = iota((CHAIN, count), 0) == place % CHAIN
    ahead_q, end_own_q, end_late_q, start_ahead_q, late_q = [
        jnp.sum(
            jnp.where(at_place, looked[k * CHAIN : (k + 1) * CHAIN], 0.0), axis=0, keepdims=True
        )
        for k in range(5)
    ]
    is_ahead = rank < ahead_q
    is_own = rank < end_own_q
    is_late = rank < end_late_q
    slot = jnp.where(
        is_ahead,
        start_ahead_q + rank,
        jnp.where(
            is_own,
            late_q + rank - ahead_q,
            jnp.where(is_late, rank - end_own_q, f32(NONE)),
        ),
    )
    shift = jnp.where(is_ahead, -1.0, jnp.where(is_own, 0.0, jnp.where(is_late, 1.0, 0.0)))
    part = jnp.where(is_ahead, 2.0, jnp.where(is_own, 0.0, jnp.where(is_late, 1.0, 0.0)))
    carrier = owner + STRIDE * shift
    entry = part * f32(SPAN) + row
    carrier_hot = (iota((devices, count), 0) == carrier.astype(i32)).astype(bf16)
    slot_line = iota((128, count), 0)
    slot_hot = jnp.logical_and(slot_line == slot.astype(i32), slot_line < SLOTS)
    rank_hot = slot_line == rank.astype(i32) + DIRECT
    entry_high, entry_low = split_int(entry, 64.0)
    row_high, row_low = split_int(row, 64.0)

    def listed(hot, places, values):
        return nt(hot, jnp.where(places, values, 0.0).astype(bf16))

    request = 64.0 * (
        listed(carrier_hot, slot_hot, entry_high) + listed(owner_hot, rank_hot, row_high)
    )
    request = request + (
        listed(carrier_hot, slot_hot, entry_low) + listed(owner_hot, rank_hot, row_low)
    )
    lane_out = iota((devices, 128), 1)
    request_ref[...] = jnp.where(lane_out == FLAG, overflow[0:1, 0:1], request)
    line_out = iota((8, count), 0)
    plan = jnp.zeros((8, count), f32)
    for k, values in enumerate((carrier, slot, rank)):
        plan = jnp.where(line_out == k, values, plan)
    plan_ref[...] = plan


def make_plan(local, other, devices):
    count = 2 * local.shape[1]
    return pl.pallas_call(
        plan_kernel,
        out_shape=(
            jax.ShapeDtypeStruct((devices, 128), f32),
            jax.ShapeDtypeStruct((8, count), f32),
            jax.ShapeDtypeStruct((8, count), f32),
        ),
        compiler_params=pltpu.CompilerParams(vmem_limit_bytes=VMEM_WHOLE),
        cost_estimate=pl.CostEstimate(flops=10**9, bytes_accessed=200000, transcendentals=0),
        name="plan",
    )(local, other)


def gather_kernel(list_ref, state_ref, own_ref, minus_ref, plus_ref, out_ref, table, sems):
    step = pl.program_id(0)
    lines = own_ref.shape[0]
    groups = out_ref.shape[0] // (8 * LINES)

    @pl.when(step == 0)
    def _():
        copies = [
            pltpu.make_async_copy(part, table.at[pl.ds(k * lines, lines)], sems.at[k])
            for k, part in enumerate((own_ref, minus_ref, plus_ref))
        ]
        for copy in copies:
            copy.start()
        for copy in copies:
            copy.wait()

    lane = iota((1, 128), 1)

    def eight(group, carry):
        start = pl.multiple_of(group * (8 * LINES), 8)
        for k in range(8):
            asker = (step * groups + group) * 8 + k
            states = jnp.zeros((1, 128), f32)
            for s in range(SLOTS):
                entry = list_ref[asker, s]
                out_ref[pl.ds(start + k * LINES + 2 * s, 2), :] = table[
                    pl.ds(pl.multiple_of(2 * entry, 2), 2), :
                ]
                states = jnp.where(lane == s, state_ref[entry], states)
            out_ref[pl.ds(start + k * LINES + 2 * SLOTS, 1), :] = states
        return carry

    lax.fori_loop(0, groups, eight, 0)


def gather_rows(lists, states, own, minus, plus):
    devices = lists.shape[0]
    chunk = 64
    smem = pl.BlockSpec(memory_space=pltpu.SMEM)
    return pl.pallas_call(
        gather_kernel,
        grid=(devices // chunk,),
        in_specs=[smem, smem] + [pl.BlockSpec(memory_space=pl.ANY)] * 3,
        out_specs=pl.BlockSpec((chunk * LINES, 128), lambda i: (i, 0)),
        out_shape=jax.ShapeDtypeStruct((devices * LINES, 128), f32),
        scratch_shapes=[pltpu.VMEM((3 * own.shape[0], 128), f32), pltpu.SemaphoreType.DMA((3,))],
        compiler_params=pltpu.CompilerParams(vmem_limit_bytes=VMEM_LIMIT),
        cost_estimate=pl.CostEstimate(flops=0, bytes_accessed=8 * 10**6, transcendentals=0),
        name="gather_rows",
    )(lists, states, own, minus, plus)


def slots_kernel(
    start_ref, meta_ref, plan_ref, near_ref, own_ref, weight_ref, scale_ref, local_ref, high, low
):
    count = meta_ref.shape[1]
    rows, total = weight_ref.shape
    width = own_ref.shape[1]
    carrier = plan_ref[0:1, :]
    slot = plan_ref[1:2, :]
    four = jnp.floor(carrier * 0.25)
    pair = jnp.floor((carrier - 4.0 * four) * 0.5)
    odd = carrier - 4.0 * four - 2.0 * pair
    key = four * (2 * PAIR) + jnp.where(
        slot < FIRST,
        odd * 16 + pair * 8 + slot,
        32 + pair * 8 + odd * (8 - REST) + slot - FIRST,
    )
    key = jnp.where(slot < SLOTS, key, -1.0).astype(i32)
    reactant, product = meta_ref[0:1, :], meta_ref[1:2, :]
    param, constant = meta_ref[6:7, :], meta_ref[7:8, :]
    near = near_ref[8:9, :]
    scaled = constant * near
    a_high, a_low = split_int(reactant, 32.0)
    c_high, c_low = split_int(product, 32.0)
    line = iota((8, count), 0)
    packed = jnp.zeros((8, count), f32)
    for k, values in enumerate(
        (a_high, a_low, c_high, c_low, meta_ref[2:3, :], meta_ref[3:4, :])
    ):
        packed = jnp.where(line == k, values, packed)
    packed = packed.astype(bf16)
    high_part, low_part = halves(own_ref[...])
    high[...] = high_part
    low[...] = low_part
    block = 256
    for start in range(0, total, block):
        hot = iota((block, count), 0) + start == key
        found = nt(packed, jnp.where(hot, 1.0, 0.0).astype(bf16))
        a = (32.0 * found[0:1] + found[1:2]).astype(i32)
        c = (32.0 * found[2:3] + found[3:4]).astype(i32)
        species = iota((rows, block), 0)
        weight = jnp.where(species == c, found[5:6], 0.0) - jnp.where(
            species == a, found[4:5], 0.0
        )
        weight_ref[:, start : start + block] = weight.astype(f8)

        def column(values):
            return jnp.sum(jnp.where(hot, values, 0.0), axis=1, keepdims=True)

        scale = column(scaled)
        scale_ref[start : start + block, :] = jnp.broadcast_to(scale, (block, 128))
        from_row = (iota((block, rows), 1) == column(reactant).astype(i32)).astype(bf16)
        chosen = iota((block, width), 1) + start_ref[0] == column(param).astype(i32)
        local_ref[start : start + block, :] = column(constant) * (
            nn(from_row, high[...]) + nn(from_row, low[...])
        ) + jnp.where(chosen, scale, 0.0)


def make_slots(start, meta, plan, near, own, devices):
    total = devices // 2 * PAIR
    rows, width = own.shape
    vmem = pl.BlockSpec(memory_space=pltpu.VMEM)
    return pl.pallas_call(
        slots_kernel,
        in_specs=[pl.BlockSpec(memory_space=pltpu.SMEM)] + [vmem] * 4,
        out_shape=(
            jax.ShapeDtypeStruct((rows, total), f8),
            jax.ShapeDtypeStruct((total, 128), f32),
            jax.ShapeDtypeStruct((total, width), f32),
        ),
        scratch_shapes=[pltpu.VMEM((rows, width), bf16)] * 2,
        compiler_params=pltpu.CompilerParams(vmem_limit_bytes=VMEM_LIMIT),
        cost_estimate=pl.CostEstimate(flops=4 * 10**9, bytes_accessed=5 * 10**6, transcendentals=0),
        name="slots",
    )(start, meta, plan, near, own)


def near_kernel(meta_ref, state_ref, out_ref):
    count = meta_ref.shape[1]
    high, low = split_int(meta_ref[0:1, :], 128.0)
    low_hot = (iota((128, count), 0) == low.astype(i32)).astype(f32)
    columns = nn(state_ref[...], low_hot, lax.Precision.HIGHEST)
    picked = jnp.where(iota((8, count), 0) == high.astype(i32), columns, 0.0)
    out_ref[0:8, :] = picked
    out_ref[8:16, :] = jnp.broadcast_to(jnp.sum(picked, axis=0, keepdims=True), (8, count))


def near_state(meta, state):
    return pl.pallas_call(
        near_kernel,
        out_shape=jax.ShapeDtypeStruct((16, meta.shape[1]), f32),
        compiler_params=pltpu.CompilerParams(vmem_limit_bytes=VMEM_LIMIT),
        name="near_state",
    )(meta, state)


def band_kernel(
    columns_ref, counts_ref, own_ref, before_ref, after_ref, blocks_ref, out_ref, high, low
):
    step = pl.program_id(0)
    rows, width = own_ref.shape
    per_step, _, size, _ = blocks_ref.shape
    edge = before_ref.shape[0] // 2

    @pl.when(step == 0)
    def _():
        for half in range(2):
            columns = slice(half * 128, (half + 1) * 128)
            for values, at in (
                (before_ref[pl.ds(half, edge, stride=2), :], 0),
                (own_ref[:, columns], edge),
                (after_ref[pl.ds(half, edge, stride=2), :], edge + rows),
            ):
                high_part, low_part = halves(values)
                high[at : at + values.shape[0], columns] = high_part
                low[at : at + values.shape[0], columns] = low_part

    for r in range(per_step):
        place = step * per_step + r

        def add_slot(k, sum_so_far):
            at = pl.multiple_of(columns_ref[place, k] * size, size)
            block_high, block_low = halves(blocks_ref[r, k])
            rows_high = high[pl.ds(at, size), :]
            rows_low = low[pl.ds(at, size), :]
            return sum_so_far + (
                nn(block_high, rows_high) + (nn(block_low, rows_high) + nn(block_high, rows_low))
            )

        band = lax.fori_loop(0, counts_ref[place], add_slot, jnp.zeros((size, width), f32))
        at = pl.multiple_of(place * size, size)
        out_ref[r * size : (r + 1) * size, :] = own_ref[pl.ds(at, size), :] + step_length * band


def band_terms(columns, counts, own, before, after, blocks):
    rows, width = own.shape
    block_rows, slots, size, _ = blocks.shape
    per_step = 2
    edge = before.shape[0] // 2

    def whole(x):
        return pl.BlockSpec(x.shape, lambda i: (0,) * x.ndim)

    smem = pl.BlockSpec(memory_space=pltpu.SMEM)
    return pl.pallas_call(
        band_kernel,
        grid=(block_rows // per_step,),
        in_specs=[smem, smem]
        + [whole(x) for x in (own, before, after)]
        + [pl.BlockSpec((per_step, slots, size, size), lambda i: (i, 0, 0, 0))],
        out_specs=pl.BlockSpec((per_step * size, width), lambda i: (i, 0)),
        out_shape=jax.ShapeDtypeStruct((rows, width), f32),
        scratch_shapes=[pltpu.VMEM((rows + 2 * edge, width), bf16)] * 2,
        compiler_params=pltpu.CompilerParams(vmem_limit_bytes=VMEM_LIMIT),
        cost_estimate=pl.CostEstimate(
            flops=3 * 10**9, bytes_accessed=7 * 10**6, transcendentals=0
        ),
        name="band_terms",
    )(columns, counts, own, before, after, blocks)


def tail_kernel(
    far_hbm,
    scale_hbm,
    local_hbm,
    weight_hbm,
    base_hbm,
    out_hbm,
    far_ref,
    scale_ref,
    local_ref,
    weight_ref,
    base_ref,
    out_ref,
    high,
    low,
    low_small,
    sems,
    out_sems,
):
    lanes = far_ref.shape[1]
    rows, total = weight_ref.shape
    carriers = far_ref.shape[0] // LINES
    parts = 4
    block = rows // parts
    slices = ((far_hbm, far_ref), (scale_hbm, scale_ref), (local_hbm, local_ref))
    first = []
    for part in range(parts):
        copies = []
        for k, (source, target) in enumerate(slices):
            size = target.shape[0] // parts
            at = pl.ds(part * size, size)
            copies.append(pltpu.make_async_copy(source.at[at], target.at[at], sems.at[part, k]))
        first.append(copies)
    second = []
    for part in range(parts):
        at = pl.ds(part * block, block)
        second.append(
            [
                pltpu.make_async_copy(weight_hbm.at[at], weight_ref.at[at], sems.at[part, 3]),
                pltpu.make_async_copy(base_hbm.at[at], base_ref.at[at], sems.at[part, 4]),
            ]
        )
    for copies in first + second:
        for copy in copies:
            copy.start()

    lane, line = iota((8, lanes), 1), iota((8, lanes), 0)
    upper = line < REST

    def eight(group, carry):
        for k in range(2):
            values = [[[], []], [[], []], [[], []]]
            states = [[], [], []]
            for pair in range(2):
                at = pl.multiple_of(group * (8 * LINES), 8) + (4 * k + 2 * pair) * LINES
                following = at + LINES
                even_states = jnp.broadcast_to(far_ref[pl.ds(at + 2 * SLOTS, 1), :], (8, lanes))
                odd_states = jnp.broadcast_to(
                    far_ref[pl.ds(following + 2 * SLOTS, 1), :], (8, lanes)
                )
                states[0].append(jnp.where(lane == line, even_states, 0.0))
                states[1].append(jnp.where(lane == line, odd_states, 0.0))
                states[2].append(
                    jnp.where(
                        upper,
                        jnp.where(lane == line + FIRST, even_states, 0.0),
                        jnp.where(lane == line + SLOTS - 8, odd_states, 0.0),
                    )
                )
                for half in range(2):
                    values[0][half].append(far_ref[pl.ds(at + half, 8, stride=2), :])
                    values[1][half].append(far_ref[pl.ds(following + half, 8, stride=2), :])
                    values[2][half].append(
                        jnp.where(
                            upper,
                            far_ref[pl.ds(at + 2 * FIRST + half, 8, stride=2), :],
                            far_ref[pl.ds(following + 2 * (SLOTS - 8) + half, 8, stride=2), :],
                        )
                    )
            for j in range(3):
                state = jnp.sum(jnp.concatenate(states[j], axis=0), axis=1, keepdims=True)
                place = pl.ds(pl.multiple_of(group * (4 * PAIR), 16) + k * 2 * PAIR + j * 16, 16)
                for half in range(2):
                    columns = slice(half * lanes, (half + 1) * lanes)
                    mixed = (
                        jnp.concatenate(values[j][half], axis=0) * scale_ref[place, :]
                        + state * local_ref[place, columns]
                    )
                    high_part = mixed.astype(bf16)
                    low_part = (mixed - high_part.astype(f32)) * LOW_SCALE
                    high[place, columns] = high_part
                    low[place, columns] = low_part.astype(bf16)
        return carry

    groups = carriers // 8 // parts
    for part in range(parts):
        for copy in first[part]:
            copy.wait()
        lax.fori_loop(part * groups, (part + 1) * groups, eight, 0)

    low_small[...] = low[...].astype(f8)
    stores = []
    for part in range(parts):
        for copy in second[part]:
            copy.wait()
        at = pl.ds(part * block, block)
        weight = weight_ref[at, :]
        sums = nn(weight.astype(bf16), high[...])
        sums = sums + nn(weight, low_small[...]) * (1.0 / LOW_SCALE)
        out_ref[at, :] = base_ref[at, :] + step_length * sums
        store = pltpu.make_async_copy(out_ref.at[at], out_hbm.at[at], out_sems.at[part])
        store.start()
        stores.append(store)
    for store in stores:
        store.wait()


def add_far(far, scale, local, weight, base):
    rows, total = weight.shape
    width = base.shape[1]
    held = [pltpu.VMEM(x.shape, x.dtype) for x in (far, scale, local, weight, base, base)]
    anywhere = pl.BlockSpec(memory_space=pl.ANY)
    return pl.pallas_call(
        tail_kernel,
        in_specs=[anywhere] * 5,
        out_specs=anywhere,
        out_shape=jax.ShapeDtypeStruct((rows, width), f32),
        scratch_shapes=held
        + [pltpu.VMEM((total, width), bf16)] * 2
        + [pltpu.VMEM((total, width), f8)]
        + [pltpu.SemaphoreType.DMA((4, 5)), pltpu.SemaphoreType.DMA((4,))],
        compiler_params=pltpu.CompilerParams(vmem_limit_bytes=VMEM_WHOLE),
        cost_estimate=pl.CostEstimate(
            flops=2 * 10**9, bytes_accessed=8 * 10**6, transcendentals=0
        ),
        name="add_far",
    )(far, scale, local, weight, base)


def exchange(x):
    return lax.all_to_all(x, "species", split_axis=0, concat_axis=0, tiled=True)


def add_overflow(result, start, meta, plan, near, direct, own, state):
    rows = exchange(own[direct])
    states = exchange(state[direct])
    owner = meta[4].astype(i32)
    rank = plan[2].astype(i32)
    reactant = meta[0].astype(i32)
    product = meta[1].astype(i32)
    constant = jnp.where(plan[1] == NONE, meta[7], 0.0)
    chosen = meta[6].astype(i32)[:, None] - start == iota((1, own.shape[1]), 1)
    growth = (constant * states[owner, rank])[:, None] * (
        own[reactant] + jnp.where(chosen, near[8][:, None], 0.0)
    ) + (constant * near[8])[:, None] * rows[owner, rank]
    result = result.at[product].add(step_length * meta[3][:, None] * growth)
    return result.at[reactant].add(-step_length * meta[2][:, None] * growth)


def body(
    species_state,
    sensitivity,
    jacobian_blocks,
    block_columns,
    block_counts,
    reaction_rows,
    stoichiometry,
    catalyst_device,
    catalyst_row,
    param_index,
    rate_constant,
):
    devices = lax.axis_size("species")
    rows, width = sensitivity.shape
    block_rows, _, size, _ = jacobian_blocks.shape
    edge = H * size
    ends = devices - 1

    place = lax.axis_index("species")
    first, last = place % STRIDE == 0, place % STRIDE == STRIDE - 1
    state_table = species_state.reshape(-1, 128)
    local_meta, table = prepare(
        reaction_rows,
        stoichiometry,
        catalyst_device,
        catalyst_row,
        param_index,
        rate_constant,
        sensitivity,
        state_table,
    )
    other_meta = lax.ppermute(local_meta, "params", [(0, 1), (1, 0)])
    onward = [(i, (i + STRIDE) % devices) for i in range(devices)]
    minus = lax.ppermute(table, "species", onward)
    plus = lax.ppermute(table, "species", [(b, a) for a, b in onward])

    request, plan, meta = make_plan(local_meta, other_meta, devices)
    asked = exchange(request)
    lists = asked[:, :SLOTS].astype(i32)
    padding = jnp.zeros((SPAN - rows,), f32)
    states = jnp.concatenate(
        [
            piece
            for lines in (state_table, minus[2 * rows :], plus[2 * rows :])
            for piece in (lines.reshape(-1), padding)
        ]
    )
    message = gather_rows(lists, states, table, minus, plus)
    far = exchange(message.reshape(devices, 1, LINES * 128)).reshape(-1, 128)

    own, lines, minus, plus, _ = lax.optimization_barrier(
        (sensitivity, table, minus, plus, message)
    )
    tail = slice(2 * (rows - edge), 2 * rows)
    head = slice(0, 2 * edge)
    onward = [(i, i // STRIDE * STRIDE + (i + 1) % STRIDE) for i in range(devices)]
    before = lax.ppermute(jnp.where(last, minus[tail], lines[tail]), "species", onward)
    after = lax.ppermute(
        jnp.where(first, plus[head], lines[head]), "species", [(b, a) for a, b in onward]
    )
    columns = block_columns - lax.axis_index("species") * block_rows + H
    near = near_state(meta, state_table)
    start = (lax.axis_index("params") * width).astype(i32).reshape(1)
    weight, scale, local = make_slots(start, meta, plan, near, own, devices)
    base = band_terms(columns, block_counts, own, before, after, jacobian_blocks)
    result = add_far(far, scale, local, weight, base)
    direct = asked[:, DIRECT : DIRECT + RANKS].astype(i32)
    return lax.cond(
        jnp.any(asked[:, FLAG] > 0),
        lambda x: add_overflow(
            x, start, meta, plan, near, direct, sensitivity, species_state
        ),
        lambda x: x,
        result,
    )


def solution(mesh):
    specs = (
        P("species"),
        P("species", "params"),
        P("species", None, None, None),
        P("species", None),
        P("species"),
        P(("species", "params"), None),
        P(("species", "params"), None),
        P(("species", "params"), None),
        P(("species", "params")),
        P(("species", "params")),
        P(("species", "params")),
    )
    return jax.shard_map(
        body, mesh=mesh, in_specs=specs, out_specs=P("species", "params"), check_vma=False
    )
```
